128 devices in a mesh: slab: 4 (over z_lo, core), space: 32 (over y, x, z_hi).
Axes of the slice: x: 4, y: 4, z: 4 (z_hi: 2, z_lo: 2; z = z_hi * 2 + z_lo), core: 2. Of those that a mesh axis runs over, the one named last changes fastest.
Arguments:
- forcing: float32 [8, 3, 4, 4, 4, 32768], P('slab', None, None, None, None, 'space'), may hold values from -6 to 6
- coefficient: float32 [32768], P('space'), may hold values from 1.5 to 4
- neighbours: int32 [6, 32768], P(None, 'space'), may hold values from 0 to 2048, as said below
- halo_faces: int32 [2, 16384], P(None, 'space'), may hold values from 0 to 1023, as said below
- time_block: float32 [3, 3], replicated, may hold values from -0.6 to 1.6
- space_block: float32 [4, 4], replicated, may hold values from -0.6 to 1.6
- stiffness: float32 [4, 4], replicated, may hold values from -0.6 to 0.6
- time_restrict: float32 [1, 3], replicated, may hold values from 0.5 to 1.5
- space_restrict: float32 [2, 4], replicated, may hold values from 0.5 to 1.5
- coarse_smoother: float32 [2, 2], replicated, may hold values from -0.8 to 1.8
Outputs:
- correction: float32 [8, 3, 4, 4, 4, 32768], P('slab', None, None, None, None, 'space')
The draws below stay inside these ranges and needn't reach their ends.
Inputs may be any that keep to these rules, and one draw needn't show every extreme that they name: `neighbours`: for element e of partition p (local numbers below 1024) and face f = -x, +x, -y, +y, -z, +z in that order: a local element of p whose opposite face is the same face with the same node order, or 1024 + m for the m-th element of the left partition's rightward list (row 1 of halo_faces), or 1536 + m for the m-th element of the right partition's leftward list (row 0), or 2048 where the face lies on the domain boundary. Ghost slots appear only for the -x face (left) and the +x face (right). `halo_faces`: row 0 lists, in local numbers, the 512 elements of a partition whose -x face touches the left partition, row 1 those whose +x face touches the right partition, each once.
All inputs are finite; a program needn't handle non-finite values.
Results may differ from the reference program's by a relative error of at most 0.00027.
Values sent between devices are 32-bit elements; how exact they have to be, the bound alone decides.
A program may use at most 128 MiB of HBM per device.

```python
import math
import jax
import jax.numpy as jnp
from jax import lax

Q = 3
P_SIZE = 4
PC = 2
SWEEPS = 3
EX = 2
EY = 8
EZ = 64
E_DEV = 1024
GHOST = 512
SLABS = 8
ELEMS = 32768
N_SPACE = 32


def mesh_tables(key):
    key_mesh = jax.random.fold_in(key, 4242)
    parts = jnp.arange(N_SPACE, dtype=jnp.int32)

    def orders(part_index):
        part_key = jax.random.fold_in(key_mesh, part_index)
        sub_keys = jax.random.split(part_key, 3)
        numbering = jax.random.permutation(sub_keys[0], E_DEV).astype(jnp.int32)
        left_order = jax.random.permutation(sub_keys[1], GHOST).astype(jnp.int32)
        right_order = jax.random.permutation(sub_keys[2], GHOST).astype(jnp.int32)
        return (numbering, left_order, right_order)
    numbering, left_order, right_order = jax.vmap(orders)(parts)
    slots = jnp.arange(GHOST, dtype=jnp.int32)

    def invert(order_row):
        return jnp.zeros((GHOST,), jnp.int32).at[order_row].set(slots)
    left_slot = jax.vmap(invert)(left_order)
    right_slot = jax.vmap(invert)(right_order)
    cells = jnp.arange(E_DEV, dtype=jnp.int32)
    layer = cells // GHOST
    within = cells % GHOST
    row_index = within // EZ
    col_index = within % EZ
    boundary = E_DEV + 2 * GHOST

    def table(part_index):
        own = numbering[part_index]

        def neighbour_of(offset):
            return own[jnp.clip(cells + offset, 0, E_DEV - 1)]
        left_part = jnp.clip(part_index - 1, 0, N_SPACE - 1)
        right_part = jnp.clip(part_index + 1, 0, N_SPACE - 1)
        minus_x = jnp.where(layer > 0, neighbour_of(-GHOST), jnp.where(part_index > 0, E_DEV + right_slot[left_part][within], boundary))
        plus_x = jnp.where(layer < EX - 1, neighbour_of(GHOST), jnp.where(part_index < N_SPACE - 1, E_DEV + GHOST + left_slot[right_part][within], boundary))
        minus_y = jnp.where(row_index > 0, neighbour_of(-EZ), boundary)
        plus_y = jnp.where(row_index < EY - 1, neighbour_of(EZ), boundary)
        minus_z = jnp.where(col_index > 0, neighbour_of(-1), boundary)
        plus_z = jnp.where(col_index < EZ - 1, neighbour_of(1), boundary)
        by_cell = jnp.stack([minus_x, plus_x, minus_y, plus_y, minus_z, plus_z]).astype(jnp.int32)
        by_local = jnp.zeros((6, E_DEV), jnp.int32).at[:, own].set(by_cell)
        sends = jnp.stack([own[left_order[part_index]], own[(EX - 1) * GHOST + right_order[part_index]]])
        return (by_local, sends.astype(jnp.int32))
    tables, send_lists = jax.vmap(table)(parts)
    neighbour_table = jnp.transpose(tables, (1, 0, 2)).reshape(6, N_SPACE * E_DEV)
    face_lists = jnp.transpose(send_lists, (1, 0, 2)).reshape(2, N_SPACE * GHOST)
    return (neighbour_table.astype(jnp.int32), face_lists.astype(jnp.int32))


def draw_neighbours(key, part):
    return mesh_tables(key)[0]


def draw_halo_faces(key, part):
    return mesh_tables(key)[1]


def near_identity(key, order, spread):
    perturbation = spread * jnp.clip(jax.random.normal(key, (order, order), jnp.float32), -4.0, 4.0)
    return jnp.eye(order, dtype=jnp.float32) + perturbation


def draw_time_block(key, part):
    return near_identity(jax.random.fold_in(key, 11), Q, 0.15)


def draw_space_block(key, part):
    return near_identity(jax.random.fold_in(key, 12), P_SIZE, 0.15)


def draw_coarse_smoother(key, part):
    return near_identity(jax.random.fold_in(key, 13), PC, 0.2)


def levels(own_key, shape, shards, least, top_value):
    def one(dim, blocks):
        steps = jax.random.uniform(jax.random.fold_in(jax.random.fold_in(own_key, 6), dim), (blocks,), jnp.float32, least / len(shards), top_value / len(shards))
        return jnp.repeat(jnp.exp(steps), shape[dim] // blocks).reshape((-1,) + (1,) * (len(shape) - dim - 1))

    gain = one(*shards[0])
    for cut in shards[1:]:
        gain = gain * one(*cut)
    return gain


def noise(stream_key, dims, scale, reach, cuts=(), kind=jnp.bfloat16):
    factor_of = levels(stream_key, dims, cuts, -0.22, 0.18) if cuts else 1.0
    values = jax.random.normal(stream_key, dims, jnp.float32) * scale * factor_of
    return jnp.minimum(jnp.maximum(values, -reach), reach).astype(kind)


def setup_inputs(seed: int = 0) -> dict:
    keys = jax.random.split(jax.random.key(seed), 11)
    forcing = noise(keys[0], (SLABS, Q, P_SIZE, P_SIZE, P_SIZE, ELEMS), 1.0, 6.0, ((0, 4), (5, 32)), jnp.float32)
    coefficient = jnp.clip(jnp.exp(math.log(4.0) - 0.98082925 * jax.random.uniform(keys[1], (ELEMS,), jnp.float32) ** levels(keys[1], (ELEMS,), ((0, 32),), -0.2, 0.2)), 1.5, 4.0)
    neighbours = draw_neighbours(jax.random.fold_in(keys[10], 71), 0)
    halo_faces = draw_halo_faces(jax.random.fold_in(keys[10], 71), 0)
    time_block = draw_time_block(jax.random.fold_in(keys[10], 71), 0)
    space_block = draw_space_block(jax.random.fold_in(keys[10], 71), 0)
    stiffness = noise(keys[6], (P_SIZE, P_SIZE), 0.1, 0.6, (), jnp.float32)
    time_restrict = jnp.clip(jax.random.uniform(keys[7], (1, Q), jnp.float32, 0.5, 1.5), 0.5, 1.5)
    space_restrict = jnp.clip(jax.random.uniform(keys[8], (PC, P_SIZE), jnp.float32, 0.5, 1.5), 0.5, 1.5)
    coarse_smoother = draw_coarse_smoother(jax.random.fold_in(keys[10], 71), 0)
    return {"forcing": forcing, "coefficient": coefficient, "neighbours": neighbours, "halo_faces": halo_faces, "time_block": time_block, "space_block": space_block, "stiffness": stiffness, "time_restrict": time_restrict, "space_restrict": space_restrict, "coarse_smoother": coarse_smoother}


HIGHEST_PRECISION = lax.Precision.HIGHEST
PENALTY = 0.3
UPWIND = 0.5
COARSE_UPWIND = 0.6


def apply_along(matrix, field_in, dim_index):
    letters = "abcdefgh"[:field_in.ndim]
    source = letters[:dim_index] + "q" + letters[dim_index + 1:]
    target = letters[:dim_index] + "p" + letters[dim_index + 1:]
    return jnp.einsum("pq," + source + "->" + target, matrix, field_in, precision=HIGHEST_PRECISION)


def space_apply(space_matrix, field_in, first_dim):
    result = field_in
    for dim_index in (first_dim, first_dim + 1, first_dim + 2):
        result = apply_along(space_matrix, result, dim_index)
    return result


def kron_apply(time_matrix, space_matrix, field_in):
    return space_apply(space_matrix, apply_along(time_matrix, field_in, 1), 2)


def stiffness_apply(stiffness, field_in):
    summed = apply_along(stiffness, field_in, 2) + apply_along(stiffness, field_in, 3)
    return summed + apply_along(stiffness, field_in, 4)


def face_trace(field_in, face_index):
    dim_index = 2 + face_index // 2
    node_index = (face_index % 2) * (field_in.shape[dim_index] - 1)
    return lax.index_in_dim(field_in, node_index, dim_index, keepdims=False)


def add_layer(field_in, values, face_index):
    dim_index = 2 + face_index // 2
    node_index = (face_index % 2) * (field_in.shape[dim_index] - 1)
    position = (slice(None),) * dim_index + (node_index,)
    return field_in.at[position].add(values)


def jacobi(values, coefficient, time_block, space_block):
    time_inverse = 2.0 * jnp.eye(time_block.shape[0], dtype=jnp.float32) - time_block
    space_inverse = 2.0 * jnp.eye(space_block.shape[0], dtype=jnp.float32) - space_block
    return kron_apply(time_inverse, space_inverse, values) / coefficient


def source_table(neighbours, halo_faces):
    elements = jnp.arange(ELEMS, dtype=jnp.int32)
    partition = elements // E_DEV
    left_part = jnp.clip(partition - 1, 0, N_SPACE - 1)
    right_part = jnp.clip(partition + 1, 0, N_SPACE - 1)
    left_slot = jnp.clip(neighbours - E_DEV, 0, GHOST - 1)
    right_slot = jnp.clip(neighbours - E_DEV - GHOST, 0, GHOST - 1)
    from_left = left_part * E_DEV + halo_faces[1][left_part * GHOST + left_slot]
    from_right = right_part * E_DEV + halo_faces[0][right_part * GHOST + right_slot]
    local_source = partition * E_DEV + jnp.clip(neighbours, 0, E_DEV - 1)
    outside = jnp.full(neighbours.shape, ELEMS, jnp.int32)
    sources = jnp.where(neighbours < E_DEV + 2 * GHOST, from_right, outside)
    sources = jnp.where(neighbours < E_DEV + GHOST, from_left, sources)
    sources = jnp.where(neighbours < E_DEV, local_source, sources)
    return sources.astype(jnp.int32)


def operate(field_in, coefficient, sources, time_block, space_block, stiffness):
    result = coefficient * kron_apply(time_block, space_block, field_in) + stiffness_apply(stiffness, field_in)
    for face_index in range(6):
        face_values = face_trace(field_in, face_index ^ 1)
        padded = jnp.concatenate([face_values, jnp.zeros(face_values.shape[:-1] + (1,), jnp.float32)], axis=-1)
        coupled = jnp.take(padded, sources[face_index], axis=-1)
        result = add_layer(result, -PENALTY * coupled, face_index)
    previous = jnp.concatenate([jnp.zeros((1,) + field_in.shape[2:], jnp.float32), field_in[:-1, -1]], axis=0)
    return result.at[:, 0].add(-UPWIND * coefficient * previous)


def reference(forcing, coefficient, neighbours, halo_faces, time_block, space_block, stiffness, time_restrict, space_restrict, coarse_smoother):
    sources = source_table(neighbours, halo_faces)
    iterate = jacobi(forcing, coefficient, time_block, space_block)
    for sweep_index in range(SWEEPS - 1):
        applied = operate(iterate, coefficient, sources, time_block, space_block, stiffness)
        iterate = iterate + jacobi(forcing - applied, coefficient, time_block, space_block)
    residual = forcing - operate(iterate, coefficient, sources, time_block, space_block, stiffness)
    coarse = kron_apply(time_restrict, space_restrict, residual)
    grouped = coarse[0::2] + coarse[1::2]

    def advance(carry_state, group_values):
        new_state = space_apply(coarse_smoother, COARSE_UPWIND * carry_state + group_values / coefficient, 1)
        return new_state, new_state

    initial = jnp.zeros(grouped.shape[1:], jnp.float32)
    final_state, states = lax.scan(advance, initial, grouped)
    spread = jnp.repeat(states, 2, axis=0)
    return iterate + kron_apply(time_restrict.T, space_restrict.T, spread)
```

```python
import functools

import jax
import jax.numpy as jnp
from jax import lax
from jax.experimental import pallas as pl
from jax.experimental.pallas import tpu as pltpu
from jax.sharding import PartitionSpec as P

PENALTY = 0.3
UPWIND = 0.5
COARSE_UPWIND = 0.6
HIGHEST = lax.Precision.HIGHEST
MESH = pl.DeviceIdType.MESH
F32 = jnp.float32
BF16 = jnp.bfloat16
ROWS = 192
TILE = 256
TERMS = 3


def split(value):
    terms = []
    for _ in range(TERMS):
        term = value.astype(BF16)
        terms.append(term)
        value = value - term.astype(F32)
    return terms


def blocks(value, rows):
    return sum(value[i * rows : (i + 1) * rows] for i in range(1, TERMS)) + value[0:rows]


def product(stack, rows, terms):
    total = None
    for i in range(TERMS - 1, -1, -1):
        out = dot(stack[0 : (TERMS - i) * rows, :], terms[i])
        for j in range(TERMS - 1 - i, -1, -1):
            piece = out[j * rows : (j + 1) * rows]
            total = piece if total is None else total + piece
    return total


def dot(a, b):
    return jnp.dot(a, b, preferred_element_type=F32)


def iotas(shape):
    return (
        lax.broadcasted_iota(jnp.int32, shape, 0),
        lax.broadcasted_iota(jnp.int32, shape, 1),
    )


def digits(index):
    return index >> 6, (index >> 4) & 3, (index >> 2) & 3, index & 3


def expand(entry, row_digit, col_digit, rows, cols):
    out = None
    for a in range(rows):
        row = None
        for b in range(cols):
            value = entry(a, b)
            row = jnp.where(col_digit == b, value, 0.0 if row is None else row)
        out = row if out is None else jnp.where(row_digit == a, row, out)
    return out


def kernel(
    n_slab,
    n_space,
    f_ref,
    c_ref,
    nb_ref,
    halo_ref,
    tb_ref,
    sb_ref,
    st_ref,
    tr_ref,
    sr_ref,
    cs_ref,
    o_ref,
    v_ref,
    w_ref,
    vt_ref,
    ft_ref,
    lhs_ref,
    hot_ref,
    pick_ref,
    ghost_hot_ref,
    kl_ref,
    j_ref,
    m3_ref,
    q_ref,
    r_ref,
    rf_ref,
    send_ref,
    recv_ref,
    prev_ref,
    send3_ref,
    recv3_ref,
    sprev3_ref,
    prev3_ref,
    offset_ref,
    coarse_ref,
    ssem,
    rsem,
    ps_sem,
    pr_sem,
    s3_sem,
    r3_sem,
    cs_sem,
    cr_sem,
):
    width = c_ref.shape[1]
    ghosts = halo_ref.shape[1]
    slab = lax.axis_index("slab")
    part = lax.axis_index("space")
    right = lax.rem(part + 1, n_space)
    left = lax.rem(part + n_space - 1, n_space)

    prev_ref[...] = jnp.zeros_like(prev_ref)
    prev3_ref[...] = jnp.zeros_like(prev3_ref)
    coarse_ref[...] = jnp.zeros_like(coarse_ref)

    barrier = pltpu.get_barrier_semaphore()
    for other in (left, right):
        pl.semaphore_signal(barrier, inc=1, device_id=(slab, other), device_id_type=MESH)
    for step in range(1, n_slab):
        pl.semaphore_signal(
            barrier,
            inc=1,
            device_id=(lax.rem(slab + step, n_slab), part),
            device_id_type=MESH,
        )

    def halo_copy(rnd, side, s):
        return pltpu.make_async_remote_copy(
            src_ref=send_ref.at[rnd, side, s],
            dst_ref=recv_ref.at[rnd, side, s],
            send_sem=ssem.at[rnd, side, s],
            recv_sem=rsem.at[rnd, side, s],
            device_id=(slab, (right, left)[side]),
            device_id_type=MESH,
        )

    def prev_copy(rnd):
        return pltpu.make_async_remote_copy(
            src_ref=v_ref.at[rnd, :, pl.ds(ROWS + 128, 64)],
            dst_ref=prev_ref.at[rnd],
            send_sem=ps_sem.at[rnd],
            recv_sem=pr_sem.at[rnd],
            device_id=(lax.rem(slab + 1, n_slab), part),
            device_id_type=MESH,
        )

    def halo3_copy(side):
        return pltpu.make_async_remote_copy(
            src_ref=send3_ref.at[side],
            dst_ref=recv3_ref.at[side],
            send_sem=s3_sem.at[side],
            recv_sem=r3_sem.at[side],
            device_id=(slab, (right, left)[side]),
            device_id_type=MESH,
        )

    prev3_copy = pltpu.make_async_remote_copy(
        src_ref=sprev3_ref,
        dst_ref=prev3_ref,
        send_sem=ps_sem.at[2],
        recv_sem=pr_sem.at[2],
        device_id=(lax.rem(slab + 1, n_slab), part),
        device_id_type=MESH,
    )

    def coarse_copy(step):
        return pltpu.make_async_remote_copy(
            src_ref=offset_ref,
            dst_ref=coarse_ref.at[step - 1],
            send_sem=cs_sem.at[step - 1],
            recv_sem=cr_sem.at[step - 1],
            device_id=(lax.rem(slab + step, n_slab), part),
            device_id_type=MESH,
        )

    coef = c_ref[...]
    inverse = 1.0 / coef

    def build_pick(k, carry):
        base = k * 64
        row = lax.broadcasted_iota(jnp.int32, (64, ghosts), 0) + base
        for side in range(2):
            listed = halo_ref[1 - side : 2 - side, :]
            pick_ref[side, pl.ds(pl.multiple_of(base, 64), 64), :] = jnp.where(
                row == listed, 1.0, 0.0
            ).astype(BF16)
        return carry

    lax.fori_loop(0, width // 64, build_pick, 0)

    ri, ci = iotas((ROWS, ROWS))
    rt, rx, ry, rz = digits(ri)
    ct, cx, cy, cz = digits(ci)

    def kron(time_entry, space_entry):
        out = expand(time_entry, rt, ct, 3, 3)
        for r, c in ((rx, cx), (ry, cy), (rz, cz)):
            out = out * expand(space_entry, r, c, 4, 4)
        return out

    def inverse_of(ref):
        return lambda a, b: (2.0 - ref[a, b]) if a == b else -ref[a, b]

    def plain(ref):
        return lambda a, b: ref[a, b]

    def store_terms(ref, value):
        rows = value.shape[0]
        for i, term in enumerate(split(value)):
            ref[i * rows : (i + 1) * rows, :] = term

    store_terms(j_ref, kron(inverse_of(tb_ref), inverse_of(sb_ref)))

    def columns(n):
        if isinstance(n, int):
            return pl.ds(n * TILE, TILE)
        return pl.ds(pl.multiple_of(n * TILE, TILE), TILE)

    def load(ref, rows, n):
        return jnp.concatenate([ref[2 * n, rows, :], ref[2 * n + 1, rows, :]], axis=1)

    def store(ref, rows, n, value):
        ref[2 * n, rows, :] = value[:, 0:128]
        ref[2 * n + 1, rows, :] = value[:, 128:256]

    def add(ref, rows, n, value):
        store(ref, rows, n, load(ref, rows, n) + value)

    def smooth(s, n, source, rnd_in, rnd_out):
        at = columns(n)
        rows = pl.ds(s * ROWS, ROWS)
        terms = split(load(w_ref, rows, n) if source is None else source[rows, at])
        if source is not None:
            for i, term in enumerate(terms):
                ft_ref[i, rows, at] = term
        update = product(j_ref, ROWS, terms) * inverse_at(at)
        if rnd_in is not None:
            update = update + load(v_ref.at[rnd_in], rows, n)
        store(v_ref.at[rnd_out], rows, n, update)
        for i, term in enumerate(split(update)):
            vt_ref[i, rows, at] = term

    def inverse_at(at):
        return 1.0 / c_ref[:, at]

    def picked_traces(rnd, s):
        for side in range(2):
            x = 3 * (1 - side)
            rows = [pl.ds(s * ROWS + t * 64 + x * 16, 16) for t in range(3)]
            lhs = jnp.concatenate([vt_ref[i, r, :] for i in range(TERMS) for r in rows], axis=0)
            send_ref[rnd, side, s] = blocks(dot(lhs, pick_ref[side]), 48)
            halo_copy(rnd, side, s).start()

    def loop(count, fn):
        def step(n, carry):
            fn(n)
            return carry

        lax.fori_loop(0, count, step, 0)

    tiles = width // TILE
    for s in (1, 0):
        loop(tiles, lambda n: smooth(s, n, f_ref, None, 0))
        if s == 1:
            pl.semaphore_wait(barrier, n_slab + 1)

            @pl.when(slab < n_slab - 1)
            def _():
                prev_copy(0).start()

        picked_traces(0, s)

    k_full = kron(plain(tb_ref), plain(sb_ref))
    same_t, same_x, same_y, same_z = rt == ct, rx == cx, ry == cy, rz == cz
    stiff = plain(st_ref)
    l_full = jnp.where(same_y & same_z, expand(stiff, rx, cx, 4, 4), 0.0)
    l_full = l_full + jnp.where(same_x & same_z, expand(stiff, ry, cy, 4, 4), 0.0)
    l_full = l_full + jnp.where(same_x & same_y, expand(stiff, rz, cz, 4, 4), 0.0)
    l_full = jnp.where(same_t, l_full, 0.0)
    store_terms(kl_ref, jnp.concatenate([k_full, l_full], axis=0))

    ci8, cj8 = iotas((8, ROWS))
    gx, gy, gz = ci8 >> 2, (ci8 >> 1) & 1, ci8 & 1
    jt, jx, jy, jz = digits(cj8)
    sr = plain(sr_ref)
    time_row = expand(lambda a, b: tr_ref[0, b], ci8 * 0, jt, 1, 3)
    by_dim = [expand(sr, g, j, 2, 4) for g, j in ((gx, jx), (gy, jy), (gz, jz))]
    restrict = time_row * by_dim[0] * by_dim[1] * by_dim[2]
    m3 = [
        jnp.dot(restrict, k_full, precision=HIGHEST, preferred_element_type=F32),
        jnp.dot(restrict, l_full, precision=HIGHEST, preferred_element_type=F32),
    ]
    for face in range(6):
        d, node = face // 2, face % 2 * 3
        at_face = expand(lambda a, b: sr_ref[a, node], (gx, gy, gz)[d], cj8 * 0, 2, 1)
        value = time_row * jnp.where((jx, jy, jz)[d] == 3 - node, at_face, 0.0)
        for other in range(3):
            if other != d:
                value = value * by_dim[other]
        m3.append(value)
    last = jnp.where(jt == 2, tr_ref[0, 0], 0.0) * by_dim[0] * by_dim[1] * by_dim[2]
    m3.append(last)
    m3.append(jnp.zeros((8, ROWS), F32))
    store_terms(m3_ref, jnp.concatenate(m3, axis=0))
    store_terms(r_ref, jnp.concatenate([restrict, jnp.zeros((8, ROWS), F32)], axis=0))
    rf = None
    for s in range(2):
        rows = pl.ds(s * ROWS, ROWS)
        term = product(r_ref, 16, [ft_ref[i, rows, :] for i in range(TERMS)])
        rf = term[0:8] if rf is None else rf + term[0:8]
    rf_ref[...] = rf

    def build_hot(k):
        base = k * 64
        row = lax.broadcasted_iota(jnp.int32, (64, width), 0) + base
        for face in range(6):
            hot_ref[face, pl.ds(pl.multiple_of(base, 64), 64), :] = jnp.where(
                row == nb_ref[face : face + 1, :], 1.0, 0.0
            ).astype(BF16)

    loop(width // 64, build_hot)

    def build_ghost(k):
        base = k * 64
        row = lax.broadcasted_iota(jnp.int32, (64, width), 0) + base
        for side in range(2):
            first = width + side * ghosts
            ghost_hot_ref[side, pl.ds(pl.multiple_of(base, 64), 64), :] = jnp.where(
                row + first == nb_ref[side : side + 1, :], 1.0, 0.0
            ).astype(BF16)

    loop(ghosts // 64, build_ghost)

    def residual_tile(rnd, s, n):
        at = columns(n)
        rows = pl.ds(s * ROWS, ROWS)
        c = c_ref[:, at]
        out = product(kl_ref, 2 * ROWS, [vt_ref[i, rows, at] for i in range(TERMS)])
        k_part, l_part = out[0:ROWS], out[ROWS:]
        store(w_ref, rows, n, f_ref[rows, at] - c * k_part - l_part)
        if s == 1:
            add(w_ref, pl.ds(ROWS, 64), n, UPWIND * c * load(v_ref.at[rnd], pl.ds(128, 64), n))

    def face_rows(face):
        d, node = face // 2, face % 2 * 3
        if d == 0:
            return [pl.ds(st * 64 + node * 16, 16) for st in range(6)]
        if d == 1:
            return [pl.ds(node * 4 + z, 24, stride=16) for z in range(4)]
        return [pl.ds(node, 96, stride=4)]

    def stage_traces(rnd, n):
        at = columns(n)
        for face in range(6):
            trace = jnp.concatenate([load(v_ref.at[rnd], r, n) for r in face_rows(face ^ 1)], axis=0)
            for i, term in enumerate(split(trace)):
                lhs_ref[face, i * 96 : (i + 1) * 96, at] = term

    def couple(face, n):
        at = columns(n)
        out = dot(lhs_ref[face], hot_ref[face, :, at])
        out = PENALTY * blocks(out, 96)
        first = 0
        for r in face_rows(face):
            add(w_ref, r, n, out[first : first + r.size])
            first += r.size

    def upwind(rnd, n):
        add(w_ref, pl.ds(0, 64), n, UPWIND * c_ref[:, columns(n)] * load(prev_ref.at[rnd], pl.ds(0, 64), n))

    def couple_ghosts(rnd, side, s, n):
        lhs = jnp.concatenate(split(recv_ref[rnd, side, s]), axis=0)
        out = PENALTY * blocks(dot(lhs, ghost_hot_ref[side, :, columns(n)]), 48)
        for t in range(3):
            r = pl.ds(s * ROWS + t * 64 + side * 48, 16)
            add(w_ref, r, n, out[16 * t : 16 * t + 16])

    for rnd in range(2):
        for s in range(2):
            loop(tiles, lambda n: residual_tile(rnd, s, n))
        loop(tiles, lambda n: stage_traces(rnd, n))
        for face in range(6):
            loop(tiles, lambda n: couple(face, n))
        for s in (1, 0):
            if s == 0:

                @pl.when(slab > 0)
                def _():
                    prev_copy(rnd).wait_recv()

                loop(tiles, lambda n: upwind(rnd, n))
            for side in range(2):
                halo_copy(rnd, side, s).wait_recv()
                loop(tiles, lambda n: couple_ghosts(rnd, side, s, n))
            loop(tiles, lambda n: smooth(s, n, None, rnd, rnd + 1))
            if rnd == 0:
                if s == 1:

                    @pl.when(slab < n_slab - 1)
                    def _():
                        prev_copy(1).start()

                picked_traces(1, s)

    ys = []
    for s in range(2):
        rows = pl.ds(s * ROWS, ROWS)
        ys.append(product(m3_ref, 80, [vt_ref[i, rows, :] for i in range(TERMS)]))
    sprev3_ref[...] = ys[1][64:72]

    @pl.when(slab < n_slab - 1)
    def _():
        prev3_copy.start()

    summed = ys[0] + ys[1]

    def narrow_terms(value):
        terms = [term.astype(F32) for term in split(value)]
        return jnp.concatenate(terms + [jnp.zeros_like(value)], axis=0).astype(BF16)

    for face in range(6):
        q_ref[:, pl.ds(face * width, width)] = narrow_terms(
            summed[16 + 8 * face : 24 + 8 * face]
        )
    for side in range(2):
        out = dot(q_ref[:, pl.ds(side * width, width)], pick_ref[side])
        send3_ref[side] = blocks(out, 8)
        halo3_copy(side).start()
    grouped = rf_ref[...] - summed[8:16]
    grouped = grouped + coef * (UPWIND * ys[0][64:72] - summed[0:8])
    local = None
    for face in range(6):
        term = dot(q_ref[:, pl.ds(face * width, width)], hot_ref[face])
        local = term if local is None else local + term
    for side in range(2):
        halo3_copy(side).wait_recv()
        local = local + dot(narrow_terms(recv3_ref[side]), ghost_hot_ref[side])
    grouped = grouped + PENALTY * blocks(local, 8)

    @pl.when(slab > 0)
    def _():
        prev3_copy.wait_recv()

    grouped = grouped + UPWIND * coef * prev3_ref[...]

    ai, aj = iotas((8, 8))
    cs = plain(cs_ref)
    smoother = expand(cs, ai >> 2, aj >> 2, 2, 2)
    smoother = smoother * expand(cs, (ai >> 1) & 1, (aj >> 1) & 1, 2, 2)
    smoother = smoother * expand(cs, ai & 1, aj & 1, 2, 2)
    offset = jnp.dot(smoother, grouped * inverse, precision=HIGHEST, preferred_element_type=F32)
    offset_ref[...] = offset
    for step in range(1, n_slab):

        @pl.when(slab < n_slab - step)
        def _():
            coarse_copy(step).start()

    for step in range(1, n_slab):

        @pl.when(slab >= step)
        def _():
            coarse_copy(step).wait_recv()

    state = coarse_ref[n_slab - 2]
    for step in range(n_slab - 2, -1, -1):
        term = coarse_ref[step - 1] if step else offset
        state = term + COARSE_UPWIND * jnp.dot(
            smoother, state, precision=HIGHEST, preferred_element_type=F32
        )

    pi, pk = iotas((ROWS, 8))
    pt, px, py, pz = digits(pi)
    spread = expand(lambda a, b: tr_ref[0, a], pt, pk * 0, 3, 1)
    for r, g in ((px, pk >> 2), (py, (pk >> 1) & 1), (pz, pk & 1)):
        spread = spread * expand(lambda a, b: sr_ref[b, a], r, g, 4, 2)
    lifted = jnp.dot(spread, state, precision=HIGHEST, preferred_element_type=F32)
    for s in range(2):
        rows = pl.ds(s * ROWS, ROWS)
        for n in range(tiles):
            o_ref[rows, columns(n)] = load(v_ref.at[2], rows, n) + lifted[:, n * TILE : n * TILE + TILE]

    for rnd in range(2):
        for side in range(2):
            for s in range(2):
                halo_copy(rnd, side, s).wait_send()
    for side in range(2):
        halo3_copy(side).wait_send()

    @pl.when(slab < n_slab - 1)
    def _():
        prev_copy(0).wait_send()
        prev_copy(1).wait_send()
        prev3_copy.wait_send()

    for step in range(1, n_slab):

        @pl.when(slab < n_slab - step)
        def _():
            coarse_copy(step).wait_send()


def body(
    forcing,
    coefficient,
    neighbours,
    halo_faces,
    time_block,
    space_block,
    stiffness,
    time_restrict,
    space_restrict,
    coarse_smoother,
):
    n_slab, n_space = lax.axis_size("slab"), lax.axis_size("space")
    width, ghosts = coefficient.shape[0], halo_faces.shape[1]
    field = (2 * ROWS, width)
    lanes = (width // 128, 2 * ROWS, 128)
    dma = pltpu.SemaphoreType.DMA
    vmem = pl.BlockSpec(memory_space=pltpu.VMEM)
    smem = pl.BlockSpec(memory_space=pltpu.SMEM)
    out = pl.pallas_call(
        functools.partial(kernel, n_slab, n_space),
        out_shape=jax.ShapeDtypeStruct(field, F32),
        in_specs=[vmem] * 4 + [smem] * 6,
        out_specs=vmem,
        scratch_shapes=[
            pltpu.VMEM((3,) + lanes, F32),
            pltpu.VMEM(lanes, F32),
            pltpu.VMEM((TERMS,) + field, BF16),
            pltpu.VMEM((TERMS,) + field, BF16),
            pltpu.VMEM((6, TERMS * 96, width), BF16),
            pltpu.VMEM((6, width, width), BF16),
            pltpu.VMEM((2, width, ghosts), BF16),
            pltpu.VMEM((2, ghosts, width), BF16),
            pltpu.VMEM((TERMS * 2 * ROWS, ROWS), BF16),
            pltpu.VMEM((TERMS * ROWS, ROWS), BF16),
            pltpu.VMEM((TERMS * 80, ROWS), BF16),
            pltpu.VMEM((32, 6 * width), BF16),
            pltpu.VMEM((TERMS * 16, ROWS), BF16),
            pltpu.VMEM((8, width), F32),
            pltpu.VMEM((2, 2, 2, 48, ghosts), F32),
            pltpu.VMEM((2, 2, 2, 48, ghosts), F32),
            pltpu.VMEM((2, width // 128, 64, 128), F32),
            pltpu.VMEM((2, 8, ghosts), F32),
            pltpu.VMEM((2, 8, ghosts), F32),
            pltpu.VMEM((8, width), F32),
            pltpu.VMEM((8, width), F32),
            pltpu.VMEM((8, width), F32),
            pltpu.VMEM((n_slab - 1, 8, width), F32),
            dma((2, 2, 2)),
            dma((2, 2, 2)),
            dma((3,)),
            dma((3,)),
            dma((2,)),
            dma((2,)),
            dma((n_slab - 1,)),
            dma((n_slab - 1,)),
        ],
        compiler_params=pltpu.CompilerParams(
            collective_id=0, has_side_effects=True, vmem_limit_bytes=58 * 1024 * 1024
        ),
        name="window",
    )(
        forcing.reshape(field),
        coefficient.reshape(1, width),
        neighbours,
        halo_faces,
        time_block,
        space_block,
        stiffness,
        time_restrict,
        space_restrict,
        coarse_smoother,
    )
    return out.reshape(forcing.shape)


def solution(mesh):
    in_specs = (
        P("slab", None, None, None, None, "space"),
        P("space"),
        P(None, "space"),
        P(None, "space"),
        P(),
        P(),
        P(),
        P(),
        P(),
        P(),
    )
    out_specs = P("slab", None, None, None, None, "space")
    return jax.shard_map(body, mesh=mesh, in_specs=in_specs, out_specs=out_specs, check_vma=False)
```

```python
import functools

import jax
import jax.numpy as jnp
from jax import lax
from jax.experimental import pallas as pl
from jax.experimental.pallas import tpu as pltpu
from jax.sharding import PartitionSpec as P

PENALTY = 0.3
UPWIND = 0.5
COARSE_UPWIND = 0.6
HIGHEST = lax.Precision.HIGHEST
MESH = pl.DeviceIdType.MESH
F32 = jnp.float32
BF16 = jnp.bfloat16
ROWS = 192
TILE = 256
TERMS = 3


def split(value):
    terms = []
    for _ in range(TERMS):
        term = value.astype(BF16)
        terms.append(term)
        value = value - term.astype(F32)
    return terms


def blocks(value, rows):
    return sum(value[i * rows : (i + 1) * rows] for i in range(1, TERMS)) + value[0:rows]


def product(stack, rows, terms):
    total = None
    for i in range(TERMS - 1, -1, -1):
        out = dot(stack[0 : (TERMS - i) * rows, :], terms[i])
        for j in range(TERMS - 1 - i, -1, -1):
            piece = out[j * rows : (j + 1) * rows]
            total = piece if total is None else total + piece
    return total


def dot(a, b):
    return jnp.dot(a, b, preferred_element_type=F32)


def iotas(shape):
    return (
        lax.broadcasted_iota(jnp.int32, shape, 0),
        lax.broadcasted_iota(jnp.int32, shape, 1),
    )


def digits(index):
    return index >> 6, (index >> 4) & 3, (index >> 2) & 3, index & 3


def expand(entry, row_digit, col_digit, rows, cols):
    out = None
    for a in range(rows):
        row = None
        for b in range(cols):
            value = entry(a, b)
            row = jnp.where(col_digit == b, value, 0.0 if row is None else row)
        out = row if out is None else jnp.where(row_digit == a, row, out)
    return out


def kernel(
    n_slab,
    n_space,
    f_ref,
    c_ref,
    nb_ref,
    halo_ref,
    tb_ref,
    sb_ref,
    st_ref,
    tr_ref,
    sr_ref,
    cs_ref,
    o_ref,
    v_ref,
    w_ref,
    vt_ref,
    ft_ref,
    lhs_ref,
    hot_ref,
    pick_ref,
    ghost_hot_ref,
    kl_ref,
    j_ref,
    m3_ref,
    q_ref,
    r_ref,
    rf_ref,
    send_ref,
    recv_ref,
    prev_ref,
    send3_ref,
    recv3_ref,
    sprev3_ref,
    prev3_ref,
    offset_ref,
    coarse_ref,
    ssem,
    rsem,
    ps_sem,
    pr_sem,
    s3_sem,
    r3_sem,
    cs_sem,
    cr_sem,
):
    width = c_ref.shape[1]
    ghosts = halo_ref.shape[1]
    slab = lax.axis_index("slab")
    part = lax.axis_index("space")
    right = lax.rem(part + 1, n_space)
    left = lax.rem(part + n_space - 1, n_space)

    prev_ref[...] = jnp.zeros_like(prev_ref)
    prev3_ref[...] = jnp.zeros_like(prev3_ref)
    coarse_ref[...] = jnp.zeros_like(coarse_ref)

    barrier = pltpu.get_barrier_semaphore()
    for other in (left, right):
        pl.semaphore_signal(barrier, inc=1, device_id=(slab, other), device_id_type=MESH)
    for step in range(1, n_slab):
        pl.semaphore_signal(
            barrier,
            inc=1,
            device_id=(lax.rem(slab + step, n_slab), part),
            device_id_type=MESH,
        )

    def halo_copy(rnd, side, s):
        return pltpu.make_async_remote_copy(
            src_ref=send_ref.at[rnd, side, s],
            dst_ref=recv_ref.at[rnd, side, s],
            send_sem=ssem.at[rnd, side, s],
            recv_sem=rsem.at[rnd, side, s],
            device_id=(slab, (right, left)[side]),
            device_id_type=MESH,
        )

    def prev_copy(rnd):
        return pltpu.make_async_remote_copy(
            src_ref=v_ref.at[rnd, :, pl.ds(ROWS + 128, 64)],
            dst_ref=prev_ref.at[rnd],
            send_sem=ps_sem.at[rnd],
            recv_sem=pr_sem.at[rnd],
            device_id=(lax.rem(slab + 1, n_slab), part),
            device_id_type=MESH,
        )

    def halo3_copy(side):
        return pltpu.make_async_remote_copy(
            src_ref=send3_ref.at[side],
            dst_ref=recv3_ref.at[side],
            send_sem=s3_sem.at[side],
            recv_sem=r3_sem.at[side],
            device_id=(slab, (right, left)[side]),
            device_id_type=MESH,
        )

    prev3_copy = pltpu.make_async_remote_copy(
        src_ref=sprev3_ref,
        dst_ref=prev3_ref,
        send_sem=ps_sem.at[2],
        recv_sem=pr_sem.at[2],
        device_id=(lax.rem(slab + 1, n_slab), part),
        device_id_type=MESH,
    )

    def coarse_copy(step):
        return pltpu.make_async_remote_copy(
            src_ref=offset_ref,
            dst_ref=coarse_ref.at[step - 1],
            send_sem=cs_sem.at[step - 1],
            recv_sem=cr_sem.at[step - 1],
            device_id=(lax.rem(slab + step, n_slab), part),
            device_id_type=MESH,
        )

    coef = c_ref[...]
    inverse = 1.0 / coef

    def build_pick(k, carry):
        base = k * 64
        row = lax.broadcasted_iota(jnp.int32, (64, ghosts), 0) + base
        for side in range(2):
            listed = halo_ref[1 - side : 2 - side, :]
            pick_ref[side, pl.ds(pl.multiple_of(base, 64), 64), :] = jnp.where(
                row == listed, 1.0, 0.0
            ).astype(BF16)
        return carry

    lax.fori_loop(0, width // 64, build_pick, 0)

    ri, ci = iotas((ROWS, ROWS))
    rt, rx, ry, rz = digits(ri)
    ct, cx, cy, cz = digits(ci)

    def kron(time_entry, space_entry):
        out = expand(time_entry, rt, ct, 3, 3)
        for r, c in ((rx, cx), (ry, cy), (rz, cz)):
            out = out * expand(space_entry, r, c, 4, 4)
        return out

    def inverse_of(ref):
        return lambda a, b: (2.0 - ref[a, b]) if a == b else -ref[a, b]

    def plain(ref):
        return lambda a, b: ref[a, b]

    def store_terms(ref, value):
        rows = value.shape[0]
        for i, term in enumerate(split(value)):
            ref[i * rows : (i + 1) * rows, :] = term

    store_terms(j_ref, kron(inverse_of(tb_ref), inverse_of(sb_ref)))

    def columns(n):
        if isinstance(n, int):
            return pl.ds(n * TILE, TILE)
        return pl.ds(pl.multiple_of(n * TILE, TILE), TILE)

    def load(ref, rows, n):
        return jnp.concatenate([ref[2 * n, rows, :], ref[2 * n + 1, rows, :]], axis=1)

    def store(ref, rows, n, value):
        ref[2 * n, rows, :] = value[:, 0:128]
        ref[2 * n + 1, rows, :] = value[:, 128:256]

    def add(ref, rows, n, value):
        store(ref, rows, n, load(ref, rows, n) + value)

    def add_wide(ref, rows, value):
        for n in range(width // TILE):
            add(ref, rows, n, value[:, n * TILE : (n + 1) * TILE])

    def smooth(s, n, source, rnd_in, rnd_out):
        at = columns(n)
        rows = pl.ds(s * ROWS, ROWS)
        terms = split(load(w_ref, rows, n) if source is None else source[rows, at])
        if source is not None:
            for i, term in enumerate(terms):
                ft_ref[i, rows, at] = term
        update = product(j_ref, ROWS, terms) * inverse_at(at)
        if rnd_in is not None:
            update = update + load(v_ref.at[rnd_in], rows, n)
        store(v_ref.at[rnd_out], rows, n, update)
        for i, term in enumerate(split(update)):
            vt_ref[i, rows, at] = term

    def inverse_at(at):
        return 1.0 / c_ref[:, at]

    def picked_traces(rnd, s):
        for side in range(2):
            x = 3 * (1 - side)
            rows = [pl.ds(s * ROWS + t * 64 + x * 16, 16) for t in range(3)]
            lhs = jnp.concatenate([vt_ref[i, r, :] for i in range(TERMS) for r in rows], axis=0)
            send_ref[rnd, side, s] = blocks(dot(lhs, pick_ref[side]), 48)
            halo_copy(rnd, side, s).start()

    def tiled(fn):
        for n in range(width // TILE):
            fn(n)

    def loop(count, fn):
        def step(n, carry):
            fn(n)
            return carry

        lax.fori_loop(0, count, step, 0)

    tiles = width // TILE
    for s in (1, 0):
        tiled(lambda n: smooth(s, n, f_ref, None, 0))
        if s == 1:
            pl.semaphore_wait(barrier, n_slab + 1)

            @pl.when(slab < n_slab - 1)
            def _():
                prev_copy(0).start()

        picked_traces(0, s)

    k_full = kron(plain(tb_ref), plain(sb_ref))
    same_t, same_x, same_y, same_z = rt == ct, rx == cx, ry == cy, rz == cz
    stiff = plain(st_ref)
    l_full = jnp.where(same_y & same_z, expand(stiff, rx, cx, 4, 4), 0.0)
    l_full = l_full + jnp.where(same_x & same_z, expand(stiff, ry, cy, 4, 4), 0.0)
    l_full = l_full + jnp.where(same_x & same_y, expand(stiff, rz, cz, 4, 4), 0.0)
    l_full = jnp.where(same_t, l_full, 0.0)
    store_terms(kl_ref, jnp.concatenate([k_full, l_full], axis=0))

    ci8, cj8 = iotas((8, ROWS))
    gx, gy, gz = ci8 >> 2, (ci8 >> 1) & 1, ci8 & 1
    jt, jx, jy, jz = digits(cj8)
    sr = plain(sr_ref)
    time_row = expand(lambda a, b: tr_ref[0, b], ci8 * 0, jt, 1, 3)
    by_dim = [expand(sr, g, j, 2, 4) for g, j in ((gx, jx), (gy, jy), (gz, jz))]
    restrict = time_row * by_dim[0] * by_dim[1] * by_dim[2]
    m3 = [
        jnp.dot(restrict, k_full, precision=HIGHEST, preferred_element_type=F32),
        jnp.dot(restrict, l_full, precision=HIGHEST, preferred_element_type=F32),
    ]
    for face in range(6):
        d, node = face // 2, face % 2 * 3
        at_face = expand(lambda a, b: sr_ref[a, node], (gx, gy, gz)[d], cj8 * 0, 2, 1)
        value = time_row * jnp.where((jx, jy, jz)[d] == 3 - node, at_face, 0.0)
        for other in range(3):
            if other != d:
                value = value * by_dim[other]
        m3.append(value)
    last = jnp.where(jt == 2, tr_ref[0, 0], 0.0) * by_dim[0] * by_dim[1] * by_dim[2]
    m3.append(last)
    m3.append(jnp.zeros((8, ROWS), F32))
    store_terms(m3_ref, jnp.concatenate(m3, axis=0))
    store_terms(r_ref, jnp.concatenate([restrict, jnp.zeros((8, ROWS), F32)], axis=0))
    rf = None
    for s in range(2):
        rows = pl.ds(s * ROWS, ROWS)
        term = product(r_ref, 16, [ft_ref[i, rows, :] for i in range(TERMS)])
        rf = term[0:8] if rf is None else rf + term[0:8]
    rf_ref[...] = rf

    def build_hot(k):
        base = k * 64
        row = lax.broadcasted_iota(jnp.int32, (64, width), 0) + base
        for face in range(6):
            hot_ref[face, pl.ds(pl.multiple_of(base, 64), 64), :] = jnp.where(
                row == nb_ref[face : face + 1, :], 1.0, 0.0
            ).astype(BF16)

    loop(width // 64, build_hot)

    def build_ghost(k):
        base = k * 64
        row = lax.broadcasted_iota(jnp.int32, (64, width), 0) + base
        for side in range(2):
            first = width + side * ghosts
            ghost_hot_ref[side, pl.ds(pl.multiple_of(base, 64), 64), :] = jnp.where(
                row + first == nb_ref[side : side + 1, :], 1.0, 0.0
            ).astype(BF16)

    loop(ghosts // 64, build_ghost)

    def residual_tile(rnd, s, n):
        at = columns(n)
        rows = pl.ds(s * ROWS, ROWS)
        c = c_ref[:, at]
        out = product(kl_ref, 2 * ROWS, [vt_ref[i, rows, at] for i in range(TERMS)])
        k_part, l_part = out[0:ROWS], out[ROWS:]
        store(w_ref, rows, n, f_ref[rows, at] - c * k_part - l_part)
        if s == 1:
            add(w_ref, pl.ds(ROWS, 64), n, UPWIND * c * load(v_ref.at[rnd], pl.ds(128, 64), n))

    def face_rows(face):
        d, node = face // 2, face % 2 * 3
        if d == 0:
            return [pl.ds(st * 64 + node * 16, 16) for st in range(6)]
        if d == 1:
            return [pl.ds(node * 4 + z, 24, stride=16) for z in range(4)]
        return [pl.ds(node, 96, stride=4)]

    def stage_traces(rnd, n):
        at = columns(n)
        for face in range(6):
            trace = jnp.concatenate([load(v_ref.at[rnd], r, n) for r in face_rows(face ^ 1)], axis=0)
            for i, term in enumerate(split(trace)):
                lhs_ref[face, i * 96 : (i + 1) * 96, at] = term

    def couple(face):
        out = PENALTY * blocks(dot(lhs_ref[face], hot_ref[face]), 96)
        first = 0
        for r in face_rows(face):
            add_wide(w_ref, r, out[first : first + r.size])
            first += r.size

    def upwind(rnd, n):
        add(w_ref, pl.ds(0, 64), n, UPWIND * c_ref[:, columns(n)] * load(prev_ref.at[rnd], pl.ds(0, 64), n))

    def couple_ghosts(rnd, side, s):
        lhs = jnp.concatenate(split(recv_ref[rnd, side, s]), axis=0)
        out = PENALTY * blocks(dot(lhs, ghost_hot_ref[side]), 48)
        for t in range(3):
            r = pl.ds(s * ROWS + t * 64 + side * 48, 16)
            add_wide(w_ref, r, out[16 * t : 16 * t + 16])

    for rnd in range(2):
        for s in range(2):
            tiled(lambda n: residual_tile(rnd, s, n))
        tiled(lambda n: stage_traces(rnd, n))
        for face in range(6):
            couple(face)
        for s in (1, 0):
            if s == 0:

                @pl.when(slab > 0)
                def _():
                    prev_copy(rnd).wait_recv()

                tiled(lambda n: upwind(rnd, n))
            for side in range(2):
                halo_copy(rnd, side, s).wait_recv()
                couple_ghosts(rnd, side, s)
            tiled(lambda n: smooth(s, n, None, rnd, rnd + 1))
            if rnd == 0:
                if s == 1:

                    @pl.when(slab < n_slab - 1)
                    def _():
                        prev_copy(1).start()

                picked_traces(1, s)

    ys = []
    for s in range(2):
        rows = pl.ds(s * ROWS, ROWS)
        ys.append(product(m3_ref, 80, [vt_ref[i, rows, :] for i in range(TERMS)]))
    sprev3_ref[...] = ys[1][64:72]

    @pl.when(slab < n_slab - 1)
    def _():
        prev3_copy.start()

    summed = ys[0] + ys[1]

    def narrow_terms(value):
        terms = [term.astype(F32) for term in split(value)]
        return jnp.concatenate(terms + [jnp.zeros_like(value)], axis=0).astype(BF16)

    for face in range(6):
        q_ref[:, pl.ds(face * width, width)] = narrow_terms(
            summed[16 + 8 * face : 24 + 8 * face]
        )
    for side in range(2):
        out = dot(q_ref[:, pl.ds(side * width, width)], pick_ref[side])
        send3_ref[side] = blocks(out, 8)
        halo3_copy(side).start()
    grouped = rf_ref[...] - summed[8:16]
    grouped = grouped + coef * (UPWIND * ys[0][64:72] - summed[0:8])
    local = None
    for face in range(6):
        term = dot(q_ref[:, pl.ds(face * width, width)], hot_ref[face])
        local = term if local is None else local + term
    for side in range(2):
        halo3_copy(side).wait_recv()
        local = local + dot(narrow_terms(recv3_ref[side]), ghost_hot_ref[side])
    grouped = grouped + PENALTY * blocks(local, 8)

    @pl.when(slab > 0)
    def _():
        prev3_copy.wait_recv()

    grouped = grouped + UPWIND * coef * prev3_ref[...]

    ai, aj = iotas((8, 8))
    cs = plain(cs_ref)
    smoother = expand(cs, ai >> 2, aj >> 2, 2, 2)
    smoother = smoother * expand(cs, (ai >> 1) & 1, (aj >> 1) & 1, 2, 2)
    smoother = smoother * expand(cs, ai & 1, aj & 1, 2, 2)
    offset = jnp.dot(smoother, grouped * inverse, precision=HIGHEST, preferred_element_type=F32)
    offset_ref[...] = offset
    for step in range(1, n_slab):

        @pl.when(slab < n_slab - step)
        def _():
            coarse_copy(step).start()

    for step in range(1, n_slab):

        @pl.when(slab >= step)
        def _():
            coarse_copy(step).wait_recv()

    state = coarse_ref[n_slab - 2]
    for step in range(n_slab - 2, -1, -1):
        term = coarse_ref[step - 1] if step else offset
        state = term + COARSE_UPWIND * jnp.dot(
            smoother, state, precision=HIGHEST, preferred_element_type=F32
        )

    pi, pk = iotas((ROWS, 8))
    pt, px, py, pz = digits(pi)
    spread = expand(lambda a, b: tr_ref[0, a], pt, pk * 0, 3, 1)
    for r, g in ((px, pk >> 2), (py, (pk >> 1) & 1), (pz, pk & 1)):
        spread = spread * expand(lambda a, b: sr_ref[b, a], r, g, 4, 2)
    lifted = jnp.dot(spread, state, precision=HIGHEST, preferred_element_type=F32)
    for s in range(2):
        rows = pl.ds(s * ROWS, ROWS)
        for n in range(tiles):
            o_ref[rows, columns(n)] = load(v_ref.at[2], rows, n) + lifted[:, n * TILE : n * TILE + TILE]

    for rnd in range(2):
        for side in range(2):
            for s in range(2):
                halo_copy(rnd, side, s).wait_send()
    for side in range(2):
        halo3_copy(side).wait_send()

    @pl.when(slab < n_slab - 1)
    def _():
        prev_copy(0).wait_send()
        prev_copy(1).wait_send()
        prev3_copy.wait_send()

    for step in range(1, n_slab):

        @pl.when(slab < n_slab - step)
        def _():
            coarse_copy(step).wait_send()


def body(
    forcing,
    coefficient,
    neighbours,
    halo_faces,
    time_block,
    space_block,
    stiffness,
    time_restrict,
    space_restrict,
    coarse_smoother,
):
    n_slab, n_space = lax.axis_size("slab"), lax.axis_size("space")
    width, ghosts = coefficient.shape[0], halo_faces.shape[1]
    field = (2 * ROWS, width)
    lanes = (width // 128, 2 * ROWS, 128)
    dma = pltpu.SemaphoreType.DMA
    vmem = pl.BlockSpec(memory_space=pltpu.VMEM)
    smem = pl.BlockSpec(memory_space=pltpu.SMEM)
    out = pl.pallas_call(
        functools.partial(kernel, n_slab, n_space),
        out_shape=jax.ShapeDtypeStruct(field, F32),
        in_specs=[vmem] * 4 + [smem] * 6,
        out_specs=vmem,
        scratch_shapes=[
            pltpu.VMEM((3,) + lanes, F32),
            pltpu.VMEM(lanes, F32),
            pltpu.VMEM((TERMS,) + field, BF16),
            pltpu.VMEM((TERMS,) + field, BF16),
            pltpu.VMEM((6, TERMS * 96, width), BF16),
            pltpu.VMEM((6, width, width), BF16),
            pltpu.VMEM((2, width, ghosts), BF16),
            pltpu.VMEM((2, ghosts, width), BF16),
            pltpu.VMEM((TERMS * 2 * ROWS, ROWS), BF16),
            pltpu.VMEM((TERMS * ROWS, ROWS), BF16),
            pltpu.VMEM((TERMS * 80, ROWS), BF16),
            pltpu.VMEM((32, 6 * width), BF16),
            pltpu.VMEM((TERMS * 16, ROWS), BF16),
            pltpu.VMEM((8, width), F32),
            pltpu.VMEM((2, 2, 2, 48, ghosts), F32),
            pltpu.VMEM((2, 2, 2, 48, ghosts), F32),
            pltpu.VMEM((2, width // 128, 64, 128), F32),
            pltpu.VMEM((2, 8, ghosts), F32),
            pltpu.VMEM((2, 8, ghosts), F32),
            pltpu.VMEM((8, width), F32),
            pltpu.VMEM((8, width), F32),
            pltpu.VMEM((8, width), F32),
            pltpu.VMEM((n_slab - 1, 8, width), F32),
            dma((2, 2, 2)),
            dma((2, 2, 2)),
            dma((3,)),
            dma((3,)),
            dma((2,)),
            dma((2,)),
            dma((n_slab - 1,)),
            dma((n_slab - 1,)),
        ],
        compiler_params=pltpu.CompilerParams(
            collective_id=0, has_side_effects=True, vmem_limit_bytes=58 * 1024 * 1024
        ),
        name="window",
    )(
        forcing.reshape(field),
        coefficient.reshape(1, width),
        neighbours,
        halo_faces,
        time_block,
        space_block,
        stiffness,
        time_restrict,
        space_restrict,
        coarse_smoother,
    )
    return out.reshape(forcing.shape)


def solution(mesh):
    in_specs = (
        P("slab", None, None, None, None, "space"),
        P("space"),
        P(None, "space"),
        P(None, "space"),
        P(),
        P(),
        P(),
        P(),
        P(),
        P(),
    )
    out_specs = P("slab", None, None, None, None, "space")
    return jax.shard_map(body, mesh=mesh, in_specs=in_specs, out_specs=out_specs, check_vma=False)
```

```python
import functools

import jax
import jax.numpy as jnp
from jax import lax
from jax.experimental import pallas as pl
from jax.experimental.pallas import tpu as pltpu
from jax.sharding import PartitionSpec as P

PENALTY = 0.3
UPWIND = 0.5
COARSE_UPWIND = 0.6
HIGHEST = lax.Precision.HIGHEST
MESH = pl.DeviceIdType.MESH
F32 = jnp.float32
BF16 = jnp.bfloat16
ROWS = 192
TILE = 256
TERMS = 3
PICKED = 2


def split(value, count=TERMS):
    terms = []
    for _ in range(count):
        term = value.astype(BF16)
        terms.append(term)
        value = value - term.astype(F32)
    return terms


def blocks(value, rows):
    count = value.shape[0] // rows
    return sum(value[i * rows : (i + 1) * rows] for i in range(1, count)) + value[0:rows]


def product(stack, rows, terms):
    total = None
    for i in range(TERMS - 1, -1, -1):
        out = dot(stack[0 : (TERMS - i) * rows, :], terms[i])
        for j in range(TERMS - 1 - i, -1, -1):
            piece = out[j * rows : (j + 1) * rows]
            total = piece if total is None else total + piece
    return total


def dot(a, b):
    return jnp.dot(a, b, preferred_element_type=F32)


def iotas(shape):
    return (
        lax.broadcasted_iota(jnp.int32, shape, 0),
        lax.broadcasted_iota(jnp.int32, shape, 1),
    )


def digits(index):
    return index >> 6, (index >> 4) & 3, (index >> 2) & 3, index & 3


def expand(entry, row_digit, col_digit, rows, cols):
    out = None
    for a in range(rows):
        row = None
        for b in range(cols):
            value = entry(a, b)
            row = jnp.where(col_digit == b, value, 0.0 if row is None else row)
        out = row if out is None else jnp.where(row_digit == a, row, out)
    return out


def kernel(
    n_slab,
    n_space,
    forcing_ref,
    c_ref,
    nb_ref,
    halo_ref,
    tb_ref,
    sb_ref,
    st_ref,
    tr_ref,
    sr_ref,
    cs_ref,
    iterate_ref,
    state_ref,
    f_ref,
    v_ref,
    w_ref,
    vt_ref,
    ft_ref,
    lhs_ref,
    hot_ref,
    pick_ref,
    ghost_hot_ref,
    kl_ref,
    j_ref,
    m3_ref,
    q_ref,
    r_ref,
    rf_ref,
    send_ref,
    recv_ref,
    prev_ref,
    send3_ref,
    recv3_ref,
    sprev3_ref,
    prev3_ref,
    offset_ref,
    coarse_ref,
    ssem,
    rsem,
    ps_sem,
    pr_sem,
    s3_sem,
    r3_sem,
    cs_sem,
    cr_sem,
    in_sem,
    out_sem,
):
    width = c_ref.shape[1]
    ghosts = halo_ref.shape[1]
    slab = lax.axis_index("slab")
    part = lax.axis_index("space")
    right = lax.rem(part + 1, n_space)
    left = lax.rem(part + n_space - 1, n_space)

    def half_copy(s, h):
        return pltpu.make_async_copy(
            forcing_ref.at[pl.ds(s * 24, 24), h],
            f_ref.at[pl.ds(s * 24, 24), pl.ds(4 * h, 4), :],
            in_sem.at[s, h],
        )

    def out_copy(s):
        rows = pl.ds(s * ROWS, ROWS)
        return pltpu.make_async_copy(
            v_ref.at[2, :, rows, :], iterate_ref.at[:, rows, :], out_sem.at[s]
        )

    for s in (1, 0):
        for h in range(2):
            half_copy(s, h).start()

    prev_ref[...] = jnp.zeros_like(prev_ref)
    prev3_ref[...] = jnp.zeros_like(prev3_ref)
    coarse_ref[...] = jnp.zeros_like(coarse_ref)

    barrier = pltpu.get_barrier_semaphore()
    for other in (left, right):
        pl.semaphore_signal(barrier, inc=1, device_id=(slab, other), device_id_type=MESH)
    for step in range(1, n_slab):
        pl.semaphore_signal(
            barrier,
            inc=1,
            device_id=(lax.rem(slab + step, n_slab), part),
            device_id_type=MESH,
        )

    def halo_copy(rnd, side, s):
        return pltpu.make_async_remote_copy(
            src_ref=send_ref.at[rnd, side, s],
            dst_ref=recv_ref.at[rnd, side, s],
            send_sem=ssem.at[rnd, side, s],
            recv_sem=rsem.at[rnd, side, s],
            device_id=(slab, (right, left)[side]),
            device_id_type=MESH,
        )

    def prev_copy(rnd):
        return pltpu.make_async_remote_copy(
            src_ref=v_ref.at[rnd, :, pl.ds(ROWS + 128, 64)],
            dst_ref=prev_ref.at[rnd],
            send_sem=ps_sem.at[rnd],
            recv_sem=pr_sem.at[rnd],
            device_id=(lax.rem(slab + 1, n_slab), part),
            device_id_type=MESH,
        )

    def halo3_copy(side):
        return pltpu.make_async_remote_copy(
            src_ref=send3_ref.at[side],
            dst_ref=recv3_ref.at[side],
            send_sem=s3_sem.at[side],
            recv_sem=r3_sem.at[side],
            device_id=(slab, (right, left)[side]),
            device_id_type=MESH,
        )

    prev3_copy = pltpu.make_async_remote_copy(
        src_ref=sprev3_ref,
        dst_ref=prev3_ref,
        send_sem=ps_sem.at[2],
        recv_sem=pr_sem.at[2],
        device_id=(lax.rem(slab + 1, n_slab), part),
        device_id_type=MESH,
    )

    def coarse_copy(step):
        return pltpu.make_async_remote_copy(
            src_ref=offset_ref,
            dst_ref=coarse_ref.at[step - 1],
            send_sem=cs_sem.at[step - 1],
            recv_sem=cr_sem.at[step - 1],
            device_id=(lax.rem(slab + step, n_slab), part),
            device_id_type=MESH,
        )

    coef = c_ref[...]
    inverse = 1.0 / coef

    def build_pick(k, carry):
        base = k * 64
        row = lax.broadcasted_iota(jnp.int32, (64, ghosts), 0) + base
        for side in range(2):
            listed = halo_ref[1 - side : 2 - side, :]
            pick_ref[side, pl.ds(pl.multiple_of(base, 64), 64), :] = jnp.where(
                row == listed, 1.0, 0.0
            ).astype(BF16)
        return carry

    lax.fori_loop(0, width // 64, build_pick, 0)

    ri, ci = iotas((ROWS, ROWS))
    rt, rx, ry, rz = digits(ri)
    ct, cx, cy, cz = digits(ci)

    def kron(time_entry, space_entry):
        out = expand(time_entry, rt, ct, 3, 3)
        for r, c in ((rx, cx), (ry, cy), (rz, cz)):
            out = out * expand(space_entry, r, c, 4, 4)
        return out

    def inverse_of(ref):
        return lambda a, b: (2.0 - ref[a, b]) if a == b else -ref[a, b]

    def plain(ref):
        return lambda a, b: ref[a, b]

    def store_terms(ref, value):
        rows = value.shape[0]
        for i, term in enumerate(split(value)):
            ref[i * rows : (i + 1) * rows, :] = term

    store_terms(j_ref, kron(inverse_of(tb_ref), inverse_of(sb_ref)))

    def columns(n):
        if isinstance(n, int):
            return pl.ds(n * TILE, TILE)
        return pl.ds(pl.multiple_of(n * TILE, TILE), TILE)

    def load(ref, rows, n):
        return jnp.concatenate([ref[2 * n, rows, :], ref[2 * n + 1, rows, :]], axis=1)

    def store(ref, rows, n, value):
        ref[2 * n, rows, :] = value[:, 0:128]
        ref[2 * n + 1, rows, :] = value[:, 128:256]

    def add(ref, rows, n, value):
        store(ref, rows, n, load(ref, rows, n) + value)

    def add_wide(ref, rows, value):
        for n in range(width // TILE):
            add(ref, rows, n, value[:, n * TILE : (n + 1) * TILE])

    def field_tile(s, at):
        return f_ref[pl.ds(s * 24, 24), :, at].reshape(ROWS, TILE)

    def smooth(s, n, source, rnd_in, rnd_out):
        at = columns(n)
        rows = pl.ds(s * ROWS, ROWS)
        terms = split(load(w_ref, rows, n) if source is None else field_tile(s, at))
        if source is not None:
            for i, term in enumerate(terms):
                ft_ref[i, rows, at] = term
        update = product(j_ref, ROWS, terms) * inverse_at(at)
        if rnd_in is not None:
            update = update + load(v_ref.at[rnd_in], rows, n)
        store(v_ref.at[rnd_out], rows, n, update)
        for i, term in enumerate(split(update)):
            vt_ref[i, rows, at] = term

    def inverse_at(at):
        return 1.0 / c_ref[:, at]

    def picked_traces(rnd, s):
        for side in range(2):
            x = 3 * (1 - side)
            rows = [pl.ds(s * ROWS + t * 64 + x * 16, 16) for t in range(3)]
            lhs = jnp.concatenate([vt_ref[i, r, :] for i in range(PICKED) for r in rows], axis=0)
            send_ref[rnd, side, s] = blocks(dot(lhs, pick_ref[side]), 48)
            halo_copy(rnd, side, s).start()

    def tiled(fn):
        for n in range(width // TILE):
            fn(n)

    def loop(count, fn):
        def step(n, carry):
            fn(n)
            return carry

        lax.fori_loop(0, count, step, 0)

    tiles = width // TILE
    for s in (1, 0):
        for h in range(2):
            half_copy(s, h).wait()
        tiled(lambda n: smooth(s, n, f_ref, None, 0))
        if s == 1:
            pl.semaphore_wait(barrier, n_slab + 1)

            @pl.when(slab < n_slab - 1)
            def _():
                prev_copy(0).start()

        picked_traces(0, s)

    k_full = kron(plain(tb_ref), plain(sb_ref))
    same_t, same_x, same_y, same_z = rt == ct, rx == cx, ry == cy, rz == cz
    stiff = plain(st_ref)
    l_full = jnp.where(same_y & same_z, expand(stiff, rx, cx, 4, 4), 0.0)
    l_full = l_full + jnp.where(same_x & same_z, expand(stiff, ry, cy, 4, 4), 0.0)
    l_full = l_full + jnp.where(same_x & same_y, expand(stiff, rz, cz, 4, 4), 0.0)
    l_full = jnp.where(same_t, l_full, 0.0)
    store_terms(kl_ref, jnp.concatenate([k_full, l_full], axis=0))

    ci8, cj8 = iotas((8, ROWS))
    gx, gy, gz = ci8 >> 2, (ci8 >> 1) & 1, ci8 & 1
    jt, jx, jy, jz = digits(cj8)
    sr = plain(sr_ref)
    time_row = expand(lambda a, b: tr_ref[0, b], ci8 * 0, jt, 1, 3)
    by_dim = [expand(sr, g, j, 2, 4) for g, j in ((gx, jx), (gy, jy), (gz, jz))]
    restrict = time_row * by_dim[0] * by_dim[1] * by_dim[2]
    m3 = [
        jnp.dot(restrict, k_full, precision=HIGHEST, preferred_element_type=F32),
        jnp.dot(restrict, l_full, precision=HIGHEST, preferred_element_type=F32),
    ]
    for face in range(6):
        d, node = face // 2, face % 2 * 3
        at_face = expand(lambda a, b: sr_ref[a, node], (gx, gy, gz)[d], cj8 * 0, 2, 1)
        value = time_row * jnp.where((jx, jy, jz)[d] == 3 - node, at_face, 0.0)
        for other in range(3):
            if other != d:
                value = value * by_dim[other]
        m3.append(value)
    last = jnp.where(jt == 2, tr_ref[0, 0], 0.0) * by_dim[0] * by_dim[1] * by_dim[2]
    m3.append(last)
    m3.append(jnp.zeros((8, ROWS), F32))
    store_terms(m3_ref, jnp.concatenate(m3, axis=0))
    store_terms(r_ref, jnp.concatenate([restrict, jnp.zeros((8, ROWS), F32)], axis=0))
    rf = None
    for s in range(2):
        rows = pl.ds(s * ROWS, ROWS)
        term = product(r_ref, 16, [ft_ref[i, rows, :] for i in range(TERMS)])
        rf = term[0:8] if rf is None else rf + term[0:8]
    rf_ref[...] = rf

    numbers = lax.broadcasted_iota(jnp.int32, (64, width), 0).astype(F32).astype(BF16)
    one, zero = jnp.ones((64, width), BF16), jnp.zeros((64, width), BF16)

    def hot_rows(index):
        index = jnp.broadcast_to(index.astype(F32), (64, width)).astype(BF16)
        return jnp.where(numbers == index, one, zero)

    def build_hot(k):
        base = k * 64
        for face in range(6):
            hot_ref[face, pl.ds(pl.multiple_of(base, 64), 64), :] = hot_rows(
                nb_ref[face : face + 1, :] - base
            )

    loop(width // 64, build_hot)

    def build_ghost(k):
        base = k * 64
        for side in range(2):
            first = width + side * ghosts
            ghost_hot_ref[side, pl.ds(pl.multiple_of(base, 64), 64), :] = hot_rows(
                nb_ref[side : side + 1, :] - (base + first)
            )

    loop(ghosts // 64, build_ghost)

    def residual_tile(rnd, s, n):
        at = columns(n)
        rows = pl.ds(s * ROWS, ROWS)
        c = c_ref[:, at]
        out = product(kl_ref, 2 * ROWS, [vt_ref[i, rows, at] for i in range(TERMS)])
        k_part, l_part = out[0:ROWS], out[ROWS:]
        store(w_ref, rows, n, field_tile(s, at) - c * k_part - l_part)
        if s == 1:
            add(w_ref, pl.ds(ROWS, 64), n, UPWIND * c * load(v_ref.at[rnd], pl.ds(128, 64), n))

    def face_rows(face):
        d, node = face // 2, face % 2 * 3
        if d == 0:
            return [pl.ds(st * 64 + node * 16, 16) for st in range(6)]
        if d == 1:
            return [pl.ds(node * 4 + z, 24, stride=16) for z in range(4)]
        return [pl.ds(node, 96, stride=4)]

    def stage_traces(rnd, n):
        at = columns(n)
        for face in range(6):
            trace = jnp.concatenate([load(v_ref.at[rnd], r, n) for r in face_rows(face ^ 1)], axis=0)
            for i, term in enumerate(split(trace, PICKED)):
                lhs_ref[face, i * 96 : (i + 1) * 96, at] = term

    def couple(face):
        out = PENALTY * blocks(dot(lhs_ref[face], hot_ref[face]), 96)
        first = 0
        for r in face_rows(face):
            add_wide(w_ref, r, out[first : first + r.size])
            first += r.size

    def upwind(rnd, n):
        add(w_ref, pl.ds(0, 64), n, UPWIND * c_ref[:, columns(n)] * load(prev_ref.at[rnd], pl.ds(0, 64), n))

    def couple_ghosts(rnd, side, s):
        lhs = jnp.concatenate(split(recv_ref[rnd, side, s], PICKED), axis=0)
        out = PENALTY * blocks(dot(lhs, ghost_hot_ref[side]), 48)
        for t in range(3):
            r = pl.ds(s * ROWS + t * 64 + side * 48, 16)
            add_wide(w_ref, r, out[16 * t : 16 * t + 16])

    for rnd in range(2):
        for s in range(2):
            tiled(lambda n: residual_tile(rnd, s, n))
        tiled(lambda n: stage_traces(rnd, n))
        for face in range(6):
            couple(face)
        for s in (1, 0):
            if s == 0:

                @pl.when(slab > 0)
                def _():
                    prev_copy(rnd).wait_recv()

                tiled(lambda n: upwind(rnd, n))
            for side in range(2):
                halo_copy(rnd, side, s).wait_recv()
                couple_ghosts(rnd, side, s)
            tiled(lambda n: smooth(s, n, None, rnd, rnd + 1))
            if rnd == 0:
                if s == 1:

                    @pl.when(slab < n_slab - 1)
                    def _():
                        prev_copy(1).start()

                picked_traces(1, s)
            else:
                out_copy(s).start()

    ys = []
    for s in range(2):
        rows = pl.ds(s * ROWS, ROWS)
        ys.append(product(m3_ref, 80, [vt_ref[i, rows, :] for i in range(TERMS)]))
    sprev3_ref[...] = ys[1][64:72]

    @pl.when(slab < n_slab - 1)
    def _():
        prev3_copy.start()

    summed = ys[0] + ys[1]

    def narrow_terms(value):
        terms = [term.astype(F32) for term in split(value)]
        return jnp.concatenate(terms + [jnp.zeros_like(value)], axis=0).astype(BF16)

    for face in range(6):
        q_ref[:, pl.ds(face * width, width)] = narrow_terms(
            summed[16 + 8 * face : 24 + 8 * face]
        )
    for side in range(2):
        out = dot(q_ref[:, pl.ds(side * width, width)], pick_ref[side])
        send3_ref[side] = blocks(out[0:24], 8)
        halo3_copy(side).start()
    grouped = rf_ref[...] - summed[8:16]
    grouped = grouped + coef * (UPWIND * ys[0][64:72] - summed[0:8])
    local = None
    for face in range(6):
        term = dot(q_ref[:, pl.ds(face * width, width)], hot_ref[face])
        local = term if local is None else local + term
    for side in range(2):
        halo3_copy(side).wait_recv()
        local = local + dot(narrow_terms(recv3_ref[side]), ghost_hot_ref[side])
    grouped = grouped + PENALTY * blocks(local[0:24], 8)

    @pl.when(slab > 0)
    def _():
        prev3_copy.wait_recv()

    grouped = grouped + UPWIND * coef * prev3_ref[...]

    ai, aj = iotas((8, 8))
    cs = plain(cs_ref)
    smoother = expand(cs, ai >> 2, aj >> 2, 2, 2)
    smoother = smoother * expand(cs, (ai >> 1) & 1, (aj >> 1) & 1, 2, 2)
    smoother = smoother * expand(cs, ai & 1, aj & 1, 2, 2)
    offset = jnp.dot(smoother, grouped * inverse, precision=HIGHEST, preferred_element_type=F32)
    offset_ref[...] = offset
    for step in range(1, n_slab):

        @pl.when(slab < n_slab - step)
        def _():
            coarse_copy(step).start()

    for step in range(1, n_slab):

        @pl.when(slab >= step)
        def _():
            coarse_copy(step).wait_recv()

    state = coarse_ref[n_slab - 2]
    for step in range(n_slab - 2, -1, -1):
        term = coarse_ref[step - 1] if step else offset
        state = term + COARSE_UPWIND * jnp.dot(
            smoother, state, precision=HIGHEST, preferred_element_type=F32
        )

    state_ref[...] = state

    for s in range(2):
        out_copy(s).wait()
    for rnd in range(2):
        for side in range(2):
            for s in range(2):
                halo_copy(rnd, side, s).wait_send()
    for side in range(2):
        halo3_copy(side).wait_send()

    @pl.when(slab < n_slab - 1)
    def _():
        prev_copy(0).wait_send()
        prev_copy(1).wait_send()
        prev3_copy.wait_send()

    for step in range(1, n_slab):

        @pl.when(slab < n_slab - step)
        def _():
            coarse_copy(step).wait_send()


def correct(v_ref, state_ref, tr_ref, sr_ref, o_ref, lifted_ref):
    @pl.when(pl.program_id(0) == 0)
    def _():
        pi, pk = iotas((ROWS, 8))
        pt, px, py, pz = digits(pi)
        spread = expand(lambda a, b: tr_ref[0, a], pt, pk * 0, 3, 1)
        for r, g in ((px, pk >> 2), (py, (pk >> 1) & 1), (pz, pk & 1)):
            spread = spread * expand(lambda a, b: sr_ref[b, a], r, g, 4, 2)
        lifted_ref[...] = jnp.dot(
            spread, state_ref[...], precision=HIGHEST, preferred_element_type=F32
        )

    for c in range(v_ref.shape[0]):
        at = pl.ds(c * 128, 128)
        o_ref[:, :, at] = (v_ref[c] + lifted_ref[:, at]).reshape(48, 4, 128)


def body(
    forcing,
    coefficient,
    neighbours,
    halo_faces,
    time_block,
    space_block,
    stiffness,
    time_restrict,
    space_restrict,
    coarse_smoother,
):
    n_slab, n_space = lax.axis_size("slab"), lax.axis_size("space")
    width, ghosts = coefficient.shape[0], halo_faces.shape[1]
    field = (2 * ROWS, width)
    lanes = (width // 128, 2 * ROWS, 128)
    dma = pltpu.SemaphoreType.DMA
    vmem = pl.BlockSpec(memory_space=pltpu.VMEM)
    hbm = pl.BlockSpec(memory_space=pl.ANY)
    smem = pl.BlockSpec(memory_space=pltpu.SMEM)
    iterate, state = pl.pallas_call(
        functools.partial(kernel, n_slab, n_space),
        out_shape=(
            jax.ShapeDtypeStruct(lanes, F32),
            jax.ShapeDtypeStruct((8, width), F32),
        ),
        in_specs=[hbm] + [vmem] * 3 + [smem] * 6,
        out_specs=(hbm, vmem),
        scratch_shapes=[
            pltpu.VMEM((48, 8, width), F32),
            pltpu.VMEM((3,) + lanes, F32),
            pltpu.VMEM(lanes, F32),
            pltpu.VMEM((TERMS,) + field, BF16),
            pltpu.VMEM((TERMS,) + field, BF16),
            pltpu.VMEM((6, PICKED * 96, width), BF16),
            pltpu.VMEM((6, width, width), BF16),
            pltpu.VMEM((2, width, ghosts), BF16),
            pltpu.VMEM((2, ghosts, width), BF16),
            pltpu.VMEM((TERMS * 2 * ROWS, ROWS), BF16),
            pltpu.VMEM((TERMS * ROWS, ROWS), BF16),
            pltpu.VMEM((TERMS * 80, ROWS), BF16),
            pltpu.VMEM((32, 6 * width), BF16),
            pltpu.VMEM((TERMS * 16, ROWS), BF16),
            pltpu.VMEM((8, width), F32),
            pltpu.VMEM((2, 2, 2, 48, ghosts), F32),
            pltpu.VMEM((2, 2, 2, 48, ghosts), F32),
            pltpu.VMEM((2, width // 128, 64, 128), F32),
            pltpu.VMEM((2, 8, ghosts), F32),
            pltpu.VMEM((2, 8, ghosts), F32),
            pltpu.VMEM((8, width), F32),
            pltpu.VMEM((8, width), F32),
            pltpu.VMEM((8, width), F32),
            pltpu.VMEM((n_slab - 1, 8, width), F32),
            dma((2, 2, 2)),
            dma((2, 2, 2)),
            dma((3,)),
            dma((3,)),
            dma((2,)),
            dma((2,)),
            dma((n_slab - 1,)),
            dma((n_slab - 1,)),
            dma((2, 2)),
            dma((2,)),
        ],
        compiler_params=pltpu.CompilerParams(
            collective_id=0, has_side_effects=True, vmem_limit_bytes=58 * 1024 * 1024
        ),
        name="window",
    )(
        forcing.reshape(48, 2, 4, width),
        coefficient.reshape(1, width),
        neighbours,
        halo_faces,
        time_block,
        space_block,
        stiffness,
        time_restrict,
        space_restrict,
        coarse_smoother,
    )
    correction = pl.pallas_call(
        correct,
        out_shape=jax.ShapeDtypeStruct((96, 4, width), F32),
        grid=(2,),
        in_specs=[
            pl.BlockSpec((width // 128, ROWS, 128), lambda s: (0, s, 0)),
            pl.BlockSpec((8, width), lambda s: (0, 0)),
            smem,
            smem,
        ],
        out_specs=pl.BlockSpec((48, 4, width), lambda s: (s, 0, 0)),
        scratch_shapes=[pltpu.VMEM((ROWS, width), F32)],
        compiler_params=pltpu.CompilerParams(vmem_limit_bytes=60 * 1024 * 1024),
        name="correct",
    )(iterate, state, time_restrict, space_restrict)
    return correction.reshape(forcing.shape)


def solution(mesh):
    in_specs = (
        P("slab", None, None, None, None, "space"),
        P("space"),
        P(None, "space"),
        P(None, "space"),
        P(),
        P(),
        P(),
        P(),
        P(),
        P(),
    )
    out_specs = P("slab", None, None, None, None, "space")
    return jax.shard_map(body, mesh=mesh, in_specs=in_specs, out_specs=out_specs, check_vma=False)
```

```python
import functools

import jax
import jax.numpy as jnp
from jax import lax
from jax.experimental import pallas as pl
from jax.experimental.pallas import tpu as pltpu
from jax.sharding import PartitionSpec as P

PENALTY = 0.3
UPWIND = 0.5
COARSE_UPWIND = 0.6
HIGHEST = lax.Precision.HIGHEST
MESH = pl.DeviceIdType.MESH
F32 = jnp.float32
BF16 = jnp.bfloat16
ROWS = 192
TILE = 256
TERMS = 3
PICKED = 2


def split(value, count=TERMS):
    terms = []
    for _ in range(count):
        term = value.astype(BF16)
        terms.append(term)
        value = value - term.astype(F32)
    return terms


def blocks(value, rows):
    count = value.shape[0] // rows
    return sum(value[i * rows : (i + 1) * rows] for i in range(1, count)) + value[0:rows]


def product(stack, rows, terms):
    total = None
    for i in range(TERMS - 1, -1, -1):
        out = dot(stack[0 : (TERMS - i) * rows, :], terms[i])
        for j in range(TERMS - 1 - i, -1, -1):
            piece = out[j * rows : (j + 1) * rows]
            total = piece if total is None else total + piece
    return total


def dot(a, b):
    return jnp.dot(a, b, preferred_element_type=F32)


def iotas(shape):
    return (
        lax.broadcasted_iota(jnp.int32, shape, 0),
        lax.broadcasted_iota(jnp.int32, shape, 1),
    )


def digits(index):
    return index >> 6, (index >> 4) & 3, (index >> 2) & 3, index & 3


def expand(entry, row_digit, col_digit, rows, cols):
    out = None
    for a in range(rows):
        row = None
        for b in range(cols):
            value = entry(a, b)
            row = jnp.where(col_digit == b, value, 0.0 if row is None else row)
        out = row if out is None else jnp.where(row_digit == a, row, out)
    return out


def kernel(
    n_slab,
    n_space,
    forcing_ref,
    c_ref,
    nb_ref,
    halo_ref,
    tb_ref,
    sb_ref,
    st_ref,
    tr_ref,
    sr_ref,
    cs_ref,
    iterate_ref,
    state_ref,
    f_ref,
    v_ref,
    w_ref,
    vt_ref,
    ft_ref,
    lhs_ref,
    hot_ref,
    pick_ref,
    ghost_hot_ref,
    kl_ref,
    j_ref,
    m3_ref,
    q_ref,
    r_ref,
    send_ref,
    recv_ref,
    prev_ref,
    send3_ref,
    recv3_ref,
    sprev3_ref,
    prev3_ref,
    offset_ref,
    coarse_ref,
    ssem,
    rsem,
    ps_sem,
    pr_sem,
    s3_sem,
    r3_sem,
    cs_sem,
    cr_sem,
    in_sem,
    out_sem,
):
    width = c_ref.shape[1]
    ghosts = halo_ref.shape[1]
    slab = lax.axis_index("slab")
    part = lax.axis_index("space")
    right = lax.rem(part + 1, n_space)
    left = lax.rem(part + n_space - 1, n_space)

    def half_copy(s, h):
        return pltpu.make_async_copy(
            forcing_ref.at[pl.ds(s * 24, 24), h],
            f_ref.at[pl.ds(s * 24, 24), pl.ds(4 * h, 4), :],
            in_sem.at[s, h],
        )

    def out_copy(s):
        rows = pl.ds(s * ROWS, ROWS)
        return pltpu.make_async_copy(
            v_ref.at[2, :, rows, :], iterate_ref.at[:, rows, :], out_sem.at[s]
        )

    for s in (1, 0):
        for h in range(2):
            half_copy(s, h).start()

    prev_ref[...] = jnp.zeros_like(prev_ref)
    prev3_ref[...] = jnp.zeros_like(prev3_ref)
    coarse_ref[...] = jnp.zeros_like(coarse_ref)

    barrier = pltpu.get_barrier_semaphore()
    for other in (left, right):
        pl.semaphore_signal(barrier, inc=1, device_id=(slab, other), device_id_type=MESH)
    for step in range(1, n_slab):
        pl.semaphore_signal(
            barrier,
            inc=1,
            device_id=(lax.rem(slab + step, n_slab), part),
            device_id_type=MESH,
        )

    def halo_copy(rnd, side, s):
        return pltpu.make_async_remote_copy(
            src_ref=send_ref.at[rnd, side, s],
            dst_ref=recv_ref.at[rnd, side, s],
            send_sem=ssem.at[rnd, side, s],
            recv_sem=rsem.at[rnd, side, s],
            device_id=(slab, (right, left)[side]),
            device_id_type=MESH,
        )

    def prev_copy(rnd):
        return pltpu.make_async_remote_copy(
            src_ref=v_ref.at[rnd, :, pl.ds(ROWS + 128, 64)],
            dst_ref=prev_ref.at[rnd],
            send_sem=ps_sem.at[rnd],
            recv_sem=pr_sem.at[rnd],
            device_id=(lax.rem(slab + 1, n_slab), part),
            device_id_type=MESH,
        )

    def halo3_copy(side):
        return pltpu.make_async_remote_copy(
            src_ref=send3_ref.at[side],
            dst_ref=recv3_ref.at[side],
            send_sem=s3_sem.at[side],
            recv_sem=r3_sem.at[side],
            device_id=(slab, (right, left)[side]),
            device_id_type=MESH,
        )

    prev3_copy = pltpu.make_async_remote_copy(
        src_ref=sprev3_ref,
        dst_ref=prev3_ref,
        send_sem=ps_sem.at[2],
        recv_sem=pr_sem.at[2],
        device_id=(lax.rem(slab + 1, n_slab), part),
        device_id_type=MESH,
    )

    def coarse_copy(step):
        return pltpu.make_async_remote_copy(
            src_ref=offset_ref,
            dst_ref=coarse_ref.at[step - 1],
            send_sem=cs_sem.at[step - 1],
            recv_sem=cr_sem.at[step - 1],
            device_id=(lax.rem(slab + step, n_slab), part),
            device_id_type=MESH,
        )

    coef = c_ref[...]
    inverse = 1.0 / coef

    def hot_rows(index):
        shape = (64, index.shape[1])
        numbers = lax.broadcasted_iota(jnp.int32, shape, 0).astype(F32).astype(BF16)
        index = jnp.broadcast_to(index.astype(F32), shape).astype(BF16)
        return jnp.where(numbers == index, jnp.ones(shape, BF16), jnp.zeros(shape, BF16))

    def build_pick(k, carry):
        base = k * 64
        for side in range(2):
            pick_ref[side, pl.ds(pl.multiple_of(base, 64), 64), :] = hot_rows(
                halo_ref[1 - side : 2 - side, :] - base
            )
        return carry

    lax.fori_loop(0, width // 64, build_pick, 0)

    ri, ci = iotas((ROWS, ROWS))
    rt, rx, ry, rz = digits(ri)
    ct, cx, cy, cz = digits(ci)

    def kron(time_entry, space_entry):
        out = expand(time_entry, rt, ct, 3, 3)
        for r, c in ((rx, cx), (ry, cy), (rz, cz)):
            out = out * expand(space_entry, r, c, 4, 4)
        return out

    def inverse_of(ref):
        return lambda a, b: (2.0 - ref[a, b]) if a == b else -ref[a, b]

    def plain(ref):
        return lambda a, b: ref[a, b]

    def store_terms(ref, value):
        rows = value.shape[0]
        for i, term in enumerate(split(value)):
            ref[i * rows : (i + 1) * rows, :] = term

    store_terms(j_ref, kron(inverse_of(tb_ref), inverse_of(sb_ref)))

    def columns(n):
        if isinstance(n, int):
            return pl.ds(n * TILE, TILE)
        return pl.ds(pl.multiple_of(n * TILE, TILE), TILE)

    def load(ref, rows, n):
        return jnp.concatenate([ref[2 * n, rows, :], ref[2 * n + 1, rows, :]], axis=1)

    def store(ref, rows, n, value):
        ref[2 * n, rows, :] = value[:, 0:128]
        ref[2 * n + 1, rows, :] = value[:, 128:256]

    def add(ref, rows, n, value):
        store(ref, rows, n, load(ref, rows, n) + value)

    def add_wide(ref, rows, value):
        for n in range(width // TILE):
            add(ref, rows, n, value[:, n * TILE : (n + 1) * TILE])

    def field_tile(s, at):
        return f_ref[pl.ds(s * 24, 24), :, at].reshape(ROWS, TILE)

    def smooth(s, n, source, rnd_in, rnd_out):
        at = columns(n)
        rows = pl.ds(s * ROWS, ROWS)
        terms = split(load(w_ref, rows, n) if source is None else field_tile(s, at))
        if source is not None:
            for i, term in enumerate(terms):
                ft_ref[i, rows, at] = term
        update = product(j_ref, ROWS, terms) * inverse_at(at)
        if rnd_in is not None:
            update = update + load(v_ref.at[rnd_in], rows, n)
        store(v_ref.at[rnd_out], rows, n, update)
        for i, term in enumerate(split(update)):
            vt_ref[i, rows, at] = term

    def inverse_at(at):
        return 1.0 / c_ref[:, at]

    def picked_traces(rnd, s):
        for side in range(2):
            x = 3 * (1 - side)
            rows = [pl.ds(s * ROWS + t * 64 + x * 16, 16) for t in range(3)]
            lhs = jnp.concatenate([vt_ref[i, r, :] for i in range(PICKED) for r in rows], axis=0)
            send_ref[rnd, side, s] = blocks(dot(lhs, pick_ref[side]), 48)
            halo_copy(rnd, side, s).start()

    def tiled(fn):
        for n in range(width // TILE):
            fn(n)

    def loop(count, fn):
        def step(n, carry):
            fn(n)
            return carry

        lax.fori_loop(0, count, step, 0)

    tiles = width // TILE
    for s in (1, 0):
        for h in range(2):
            half_copy(s, h).wait()
        tiled(lambda n: smooth(s, n, f_ref, None, 0))
        if s == 1:
            pl.semaphore_wait(barrier, n_slab + 1)

            @pl.when(slab < n_slab - 1)
            def _():
                prev_copy(0).start()

        picked_traces(0, s)

    k_full = kron(plain(tb_ref), plain(sb_ref))
    same_t, same_x, same_y, same_z = rt == ct, rx == cx, ry == cy, rz == cz
    stiff = plain(st_ref)
    l_full = jnp.where(same_y & same_z, expand(stiff, rx, cx, 4, 4), 0.0)
    l_full = l_full + jnp.where(same_x & same_z, expand(stiff, ry, cy, 4, 4), 0.0)
    l_full = l_full + jnp.where(same_x & same_y, expand(stiff, rz, cz, 4, 4), 0.0)
    l_full = jnp.where(same_t, l_full, 0.0)
    store_terms(kl_ref, jnp.concatenate([k_full, l_full], axis=0))

    ci8, cj8 = iotas((8, ROWS))
    gx, gy, gz = ci8 >> 2, (ci8 >> 1) & 1, ci8 & 1
    jt, jx, jy, jz = digits(cj8)
    sr = plain(sr_ref)
    time_row = expand(lambda a, b: tr_ref[0, b], ci8 * 0, jt, 1, 3)
    by_dim = [expand(sr, g, j, 2, 4) for g, j in ((gx, jx), (gy, jy), (gz, jz))]
    restrict = time_row * by_dim[0] * by_dim[1] * by_dim[2]
    m3 = [
        jnp.dot(restrict, k_full, precision=HIGHEST, preferred_element_type=F32),
        jnp.dot(restrict, l_full, precision=HIGHEST, preferred_element_type=F32),
    ]
    for face in range(6):
        d, node = face // 2, face % 2 * 3
        at_face = expand(lambda a, b: sr_ref[a, node], (gx, gy, gz)[d], cj8 * 0, 2, 1)
        value = time_row * jnp.where((jx, jy, jz)[d] == 3 - node, at_face, 0.0)
        for other in range(3):
            if other != d:
                value = value * by_dim[other]
        m3.append(value)
    last = jnp.where(jt == 2, tr_ref[0, 0], 0.0) * by_dim[0] * by_dim[1] * by_dim[2]
    m3.append(last)
    m3.append(jnp.zeros((8, ROWS), F32))
    store_terms(m3_ref, jnp.concatenate(m3, axis=0))
    store_terms(r_ref, jnp.concatenate([restrict, jnp.zeros((8, ROWS), F32)], axis=0))

    def build_hot(k):
        base = k * 64
        for face in range(6):
            hot_ref[face, pl.ds(pl.multiple_of(base, 64), 64), :] = hot_rows(
                nb_ref[face : face + 1, :] - base
            )

    loop(width // 64, build_hot)

    def build_ghost(k):
        base = k * 64
        for side in range(2):
            first = width + side * ghosts
            ghost_hot_ref[side, pl.ds(pl.multiple_of(base, 64), 64), :] = hot_rows(
                nb_ref[side : side + 1, :] - (base + first)
            )

    loop(ghosts // 64, build_ghost)

    def residual_tile(rnd, s, n):
        at = columns(n)
        rows = pl.ds(s * ROWS, ROWS)
        c = c_ref[:, at]
        out = product(kl_ref, 2 * ROWS, [vt_ref[i, rows, at] for i in range(TERMS)])
        k_part, l_part = out[0:ROWS], out[ROWS:]
        store(w_ref, rows, n, field_tile(s, at) - c * k_part - l_part)
        if s == 1:
            add(w_ref, pl.ds(ROWS, 64), n, UPWIND * c * load(v_ref.at[rnd], pl.ds(128, 64), n))

    def face_rows(face):
        d, node = face // 2, face % 2 * 3
        if d == 0:
            return [pl.ds(st * 64 + node * 16, 16) for st in range(6)]
        if d == 1:
            return [pl.ds(node * 4 + z, 24, stride=16) for z in range(4)]
        return [pl.ds(node, 96, stride=4)]

    def stage_traces(rnd, n):
        at = columns(n)
        for face in range(6):
            trace = jnp.concatenate([load(v_ref.at[rnd], r, n) for r in face_rows(face ^ 1)], axis=0)
            for i, term in enumerate(split(trace, PICKED)):
                lhs_ref[face, i * 96 : (i + 1) * 96, at] = term

    def couple(face):
        out = PENALTY * blocks(dot(lhs_ref[face], hot_ref[face]), 96)
        first = 0
        for r in face_rows(face):
            add_wide(w_ref, r, out[first : first + r.size])
            first += r.size

    def upwind(rnd, n):
        add(w_ref, pl.ds(0, 64), n, UPWIND * c_ref[:, columns(n)] * load(prev_ref.at[rnd], pl.ds(0, 64), n))

    def couple_ghosts(rnd, side, s):
        lhs = jnp.concatenate(split(recv_ref[rnd, side, s], PICKED), axis=0)
        out = PENALTY * blocks(dot(lhs, ghost_hot_ref[side]), 48)
        for t in range(3):
            r = pl.ds(s * ROWS + t * 64 + side * 48, 16)
            add_wide(w_ref, r, out[16 * t : 16 * t + 16])

    ys = {}
    for rnd in range(2):
        for s in range(2):
            tiled(lambda n: residual_tile(rnd, s, n))
        tiled(lambda n: stage_traces(rnd, n))
        for face in range(6):
            couple(face)
        for s in (1, 0):
            if s == 0:

                @pl.when(slab > 0)
                def _():
                    prev_copy(rnd).wait_recv()

                tiled(lambda n: upwind(rnd, n))
            for side in range(2):
                halo_copy(rnd, side, s).wait_recv()
                couple_ghosts(rnd, side, s)
            tiled(lambda n: smooth(s, n, None, rnd, rnd + 1))
            if rnd == 0:
                if s == 1:

                    @pl.when(slab < n_slab - 1)
                    def _():
                        prev_copy(1).start()

                picked_traces(1, s)
            else:
                out_copy(s).start()
                rows = pl.ds(s * ROWS, ROWS)
                ys[s] = product(m3_ref, 80, [vt_ref[i, rows, :] for i in range(TERMS)])
                if s == 1:
                    sprev3_ref[...] = ys[1][64:72]

                    @pl.when(slab < n_slab - 1)
                    def _():
                        prev3_copy.start()

    summed = ys[0] + ys[1]

    def narrow_terms(value):
        terms = [term.astype(F32) for term in split(value)]
        return jnp.concatenate(terms + [jnp.zeros_like(value)], axis=0).astype(BF16)

    for face in range(6):
        q_ref[:, pl.ds(face * width, width)] = narrow_terms(
            summed[16 + 8 * face : 24 + 8 * face]
        )
    for side in range(2):
        out = dot(q_ref[:, pl.ds(side * width, width)], pick_ref[side])
        send3_ref[side] = blocks(out[0:24], 8)
        halo3_copy(side).start()
    rf = None
    for s in range(2):
        rows = pl.ds(s * ROWS, ROWS)
        term = product(r_ref, 16, [ft_ref[i, rows, :] for i in range(TERMS)])
        rf = term[0:8] if rf is None else rf + term[0:8]
    grouped = rf - summed[8:16]
    grouped = grouped + coef * (UPWIND * ys[0][64:72] - summed[0:8])
    local = None
    for face in range(6):
        term = dot(q_ref[:, pl.ds(face * width, width)], hot_ref[face])
        local = term if local is None else local + term
    for side in range(2):
        halo3_copy(side).wait_recv()
        local = local + dot(narrow_terms(recv3_ref[side]), ghost_hot_ref[side])
    grouped = grouped + PENALTY * blocks(local[0:24], 8)

    @pl.when(slab > 0)
    def _():
        prev3_copy.wait_recv()

    grouped = grouped + UPWIND * coef * prev3_ref[...]

    ai, aj = iotas((8, 8))
    cs = plain(cs_ref)
    smoother = expand(cs, ai >> 2, aj >> 2, 2, 2)
    smoother = smoother * expand(cs, (ai >> 1) & 1, (aj >> 1) & 1, 2, 2)
    smoother = smoother * expand(cs, ai & 1, aj & 1, 2, 2)
    offset = jnp.dot(smoother, grouped * inverse, precision=HIGHEST, preferred_element_type=F32)
    offset_ref[...] = offset
    for step in range(1, n_slab):

        @pl.when(slab < n_slab - step)
        def _():
            coarse_copy(step).start()

    for step in range(1, n_slab):

        @pl.when(slab >= step)
        def _():
            coarse_copy(step).wait_recv()

    state = coarse_ref[n_slab - 2]
    for step in range(n_slab - 2, -1, -1):
        term = coarse_ref[step - 1] if step else offset
        state = term + COARSE_UPWIND * jnp.dot(
            smoother, state, precision=HIGHEST, preferred_element_type=F32
        )

    state_ref[...] = state

    for s in range(2):
        out_copy(s).wait()
    for rnd in range(2):
        for side in range(2):
            for s in range(2):
                halo_copy(rnd, side, s).wait_send()
    for side in range(2):
        halo3_copy(side).wait_send()

    @pl.when(slab < n_slab - 1)
    def _():
        prev_copy(0).wait_send()
        prev_copy(1).wait_send()
        prev3_copy.wait_send()

    for step in range(1, n_slab):

        @pl.when(slab < n_slab - step)
        def _():
            coarse_copy(step).wait_send()


def correct(v_ref, coarse_ref, tr_ref, sr_ref, o_ref, state_ref, in_ref, sum_ref, state_sem, in_sem, out_sem):
    def in_copy(s):
        rows = pl.ds(s * ROWS, ROWS)
        return pltpu.make_async_copy(v_ref.at[:, rows, :], in_ref.at[:, rows, :], in_sem.at[s])

    def out_copy(s, h):
        return pltpu.make_async_copy(
            sum_ref.at[pl.ds(s * 24, 24), pl.ds(4 * h, 4), :],
            o_ref.at[pl.ds(s * 24, 24), h],
            out_sem.at[s, h],
        )

    state_copy = pltpu.make_async_copy(coarse_ref, state_ref, state_sem.at[0])
    state_copy.start()
    for s in range(2):
        in_copy(s).start()
    pi, pk = iotas((ROWS, 8))
    pt, px, py, pz = digits(pi)
    spread = expand(lambda a, b: tr_ref[0, a], pt, pk * 0, 3, 1)
    for r, g in ((px, pk >> 2), (py, (pk >> 1) & 1), (pz, pk & 1)):
        spread = spread * expand(lambda a, b: sr_ref[b, a], r, g, 4, 2)
    state_copy.wait()
    lifted = jnp.dot(spread, state_ref[...], precision=HIGHEST, preferred_element_type=F32)
    for s in range(2):
        in_copy(s).wait()
        for c in range(v_ref.shape[0]):
            at = slice(c * 128, c * 128 + 128)
            total = in_ref[c, s * ROWS : (s + 1) * ROWS, :] + lifted[:, at]
            sum_ref[s * 24 : (s + 1) * 24, :, at] = total.reshape(24, 8, 128)
        for h in range(2):
            out_copy(s, h).start()
    for s in range(2):
        for h in range(2):
            out_copy(s, h).wait()


def body(
    forcing,
    coefficient,
    neighbours,
    halo_faces,
    time_block,
    space_block,
    stiffness,
    time_restrict,
    space_restrict,
    coarse_smoother,
):
    n_slab, n_space = lax.axis_size("slab"), lax.axis_size("space")
    width, ghosts = coefficient.shape[0], halo_faces.shape[1]
    field = (2 * ROWS, width)
    lanes = (width // 128, 2 * ROWS, 128)
    dma = pltpu.SemaphoreType.DMA
    vmem = pl.BlockSpec(memory_space=pltpu.VMEM)
    hbm = pl.BlockSpec(memory_space=pl.ANY)
    smem = pl.BlockSpec(memory_space=pltpu.SMEM)
    iterate, state = pl.pallas_call(
        functools.partial(kernel, n_slab, n_space),
        out_shape=(
            jax.ShapeDtypeStruct(lanes, F32),
            jax.ShapeDtypeStruct((8, width), F32),
        ),
        in_specs=[hbm] + [vmem] * 3 + [smem] * 6,
        out_specs=(hbm, vmem),
        scratch_shapes=[
            pltpu.VMEM((48, 8, width), F32),
            pltpu.VMEM((3,) + lanes, F32),
            pltpu.VMEM(lanes, F32),
            pltpu.VMEM((TERMS,) + field, BF16),
            pltpu.VMEM((TERMS,) + field, BF16),
            pltpu.VMEM((6, PICKED * 96, width), BF16),
            pltpu.VMEM((6, width, width), BF16),
            pltpu.VMEM((2, width, ghosts), BF16),
            pltpu.VMEM((2, ghosts, width), BF16),
            pltpu.VMEM((TERMS * 2 * ROWS, ROWS), BF16),
            pltpu.VMEM((TERMS * ROWS, ROWS), BF16),
            pltpu.VMEM((TERMS * 80, ROWS), BF16),
            pltpu.VMEM((32, 6 * width), BF16),
            pltpu.VMEM((TERMS * 16, ROWS), BF16),
            pltpu.VMEM((2, 2, 2, 48, ghosts), F32),
            pltpu.VMEM((2, 2, 2, 48, ghosts), F32),
            pltpu.VMEM((2, width // 128, 64, 128), F32),
            pltpu.VMEM((2, 8, ghosts), F32),
            pltpu.VMEM((2, 8, ghosts), F32),
            pltpu.VMEM((8, width), F32),
            pltpu.VMEM((8, width), F32),
            pltpu.VMEM((8, width), F32),
            pltpu.VMEM((n_slab - 1, 8, width), F32),
            dma((2, 2, 2)),
            dma((2, 2, 2)),
            dma((3,)),
            dma((3,)),
            dma((2,)),
            dma((2,)),
            dma((n_slab - 1,)),
            dma((n_slab - 1,)),
            dma((2, 2)),
            dma((2,)),
        ],
        compiler_params=pltpu.CompilerParams(
            collective_id=0, has_side_effects=True, vmem_limit_bytes=58 * 1024 * 1024
        ),
        name="window",
    )(
        forcing.reshape(48, 2, 4, width),
        coefficient.reshape(1, width),
        neighbours,
        halo_faces,
        time_block,
        space_block,
        stiffness,
        time_restrict,
        space_restrict,
        coarse_smoother,
    )
    correction = pl.pallas_call(
        correct,
        out_shape=jax.ShapeDtypeStruct((48, 2, 4, width), F32),
        in_specs=[hbm, hbm, smem, smem],
        out_specs=hbm,
        scratch_shapes=[
            pltpu.VMEM((8, width), F32),
            pltpu.VMEM(lanes, F32),
            pltpu.VMEM((48, 8, width), F32),
            dma((1,)),
            dma((2,)),
            dma((2, 2)),
        ],
        compiler_params=pltpu.CompilerParams(vmem_limit_bytes=60 * 1024 * 1024),
        name="correct",
    )(iterate, state, time_restrict, space_restrict)
    return correction.reshape(forcing.shape)


def solution(mesh):
    in_specs = (
        P("slab", None, None, None, None, "space"),
        P("space"),
        P(None, "space"),
        P(None, "space"),
        P(),
        P(),
        P(),
        P(),
        P(),
        P(),
    )
    out_specs = P("slab", None, None, None, None, "space")
    return jax.shard_map(body, mesh=mesh, in_specs=in_specs, out_specs=out_specs, check_vma=False)
```

```python
import functools

import jax
import jax.numpy as jnp
from jax import lax
from jax.experimental import pallas as pl
from jax.experimental.pallas import tpu as pltpu
from jax.sharding import PartitionSpec as P

PENALTY = 0.3
UPWIND = 0.5
COARSE_UPWIND = 0.6
HIGHEST = lax.Precision.HIGHEST
MESH = pl.DeviceIdType.MESH
F32 = jnp.float32
BF16 = jnp.bfloat16
ROWS = 192
TILE = 256
TERMS = 3
PICKED = 2


def split(value, count=TERMS):
    terms = []
    for _ in range(count):
        term = value.astype(BF16)
        terms.append(term)
        value = value - term.astype(F32)
    return terms


def blocks(value, rows):
    count = value.shape[0] // rows
    return sum(value[i * rows : (i + 1) * rows] for i in range(1, count)) + value[0:rows]


def product(stack, rows, terms):
    total = None
    for i in range(TERMS - 1, -1, -1):
        out = dot(stack[0 : (TERMS - i) * rows, :], terms[i])
        for j in range(TERMS - 1 - i, -1, -1):
            piece = out[j * rows : (j + 1) * rows]
            total = piece if total is None else total + piece
    return total


def dot(a, b):
    return jnp.dot(a, b, preferred_element_type=F32)


def iotas(shape):
    return (
        lax.broadcasted_iota(jnp.int32, shape, 0),
        lax.broadcasted_iota(jnp.int32, shape, 1),
    )


def digits(index):
    return index >> 6, (index >> 4) & 3, (index >> 2) & 3, index & 3


def expand(entry, row_digit, col_digit, rows, cols):
    out = None
    for a in range(rows):
        row = None
        for b in range(cols):
            value = entry(a, b)
            row = jnp.where(col_digit == b, value, 0.0 if row is None else row)
        out = row if out is None else jnp.where(row_digit == a, row, out)
    return out


def kernel(
    n_slab,
    n_space,
    forcing_ref,
    c_ref,
    nb_ref,
    halo_ref,
    tb_ref,
    sb_ref,
    st_ref,
    tr_ref,
    sr_ref,
    cs_ref,
    iterate_ref,
    state_ref,
    f_ref,
    v_ref,
    w_ref,
    vt_ref,
    ft_ref,
    lhs_ref,
    hot_ref,
    pick_ref,
    ghost_hot_ref,
    kl_ref,
    j_ref,
    m3_ref,
    q_ref,
    r_ref,
    send_ref,
    recv_ref,
    prev_ref,
    send3_ref,
    recv3_ref,
    sprev3_ref,
    prev3_ref,
    offset_ref,
    coarse_ref,
    ssem,
    rsem,
    ps_sem,
    pr_sem,
    s3_sem,
    r3_sem,
    cs_sem,
    cr_sem,
    in_sem,
    out_sem,
):
    width = c_ref.shape[1]
    ghosts = halo_ref.shape[1]
    slab = lax.axis_index("slab")
    part = lax.axis_index("space")
    right = lax.rem(part + 1, n_space)
    left = lax.rem(part + n_space - 1, n_space)

    def half_copy(s, h):
        return pltpu.make_async_copy(
            forcing_ref.at[pl.ds(s * 24, 24), h],
            f_ref.at[pl.ds(s * 24, 24), pl.ds(4 * h, 4), :],
            in_sem.at[s, h],
        )

    def out_copy(s):
        rows = pl.ds(s * ROWS, ROWS)
        return pltpu.make_async_copy(
            v_ref.at[2, :, rows, :], iterate_ref.at[:, rows, :], out_sem.at[s]
        )

    for s in (1, 0):
        for h in range(2):
            half_copy(s, h).start()

    prev_ref[...] = jnp.zeros_like(prev_ref)
    prev3_ref[...] = jnp.zeros_like(prev3_ref)
    coarse_ref[...] = jnp.zeros_like(coarse_ref)

    barrier = pltpu.get_barrier_semaphore()
    for other in (left, right):
        pl.semaphore_signal(barrier, inc=1, device_id=(slab, other), device_id_type=MESH)
    for step in range(1, n_slab):
        pl.semaphore_signal(
            barrier,
            inc=1,
            device_id=(lax.rem(slab + step, n_slab), part),
            device_id_type=MESH,
        )

    def halo_copy(rnd, side, s):
        return pltpu.make_async_remote_copy(
            src_ref=send_ref.at[rnd, side, s],
            dst_ref=recv_ref.at[rnd, side, s],
            send_sem=ssem.at[rnd, side, s],
            recv_sem=rsem.at[rnd, side, s],
            device_id=(slab, (right, left)[side]),
            device_id_type=MESH,
        )

    def prev_copy(rnd):
        return pltpu.make_async_remote_copy(
            src_ref=v_ref.at[rnd, :, pl.ds(ROWS + 128, 64)],
            dst_ref=prev_ref.at[rnd],
            send_sem=ps_sem.at[rnd],
            recv_sem=pr_sem.at[rnd],
            device_id=(lax.rem(slab + 1, n_slab), part),
            device_id_type=MESH,
        )

    def halo3_copy(side):
        return pltpu.make_async_remote_copy(
            src_ref=send3_ref.at[side],
            dst_ref=recv3_ref.at[side],
            send_sem=s3_sem.at[side],
            recv_sem=r3_sem.at[side],
            device_id=(slab, (right, left)[side]),
            device_id_type=MESH,
        )

    prev3_copy = pltpu.make_async_remote_copy(
        src_ref=sprev3_ref,
        dst_ref=prev3_ref,
        send_sem=ps_sem.at[2],
        recv_sem=pr_sem.at[2],
        device_id=(lax.rem(slab + 1, n_slab), part),
        device_id_type=MESH,
    )

    def coarse_copy(step):
        return pltpu.make_async_remote_copy(
            src_ref=offset_ref,
            dst_ref=coarse_ref.at[step - 1],
            send_sem=cs_sem.at[step - 1],
            recv_sem=cr_sem.at[step - 1],
            device_id=(lax.rem(slab + step, n_slab), part),
            device_id_type=MESH,
        )

    coef = c_ref[...]
    inverse = 1.0 / coef

    def hot_rows(index):
        shape = (64, index.shape[1])
        numbers = lax.broadcasted_iota(jnp.int32, shape, 0).astype(F32).astype(BF16)
        index = jnp.broadcast_to(index.astype(F32), shape).astype(BF16)
        return jnp.where(numbers == index, jnp.ones(shape, BF16), jnp.zeros(shape, BF16))

    def build_pick(k, carry):
        base = k * 64
        for side in range(2):
            pick_ref[side, pl.ds(pl.multiple_of(base, 64), 64), :] = hot_rows(
                halo_ref[1 - side : 2 - side, :] - base
            )
        return carry

    lax.fori_loop(0, width // 64, build_pick, 0)

    ri, ci = iotas((ROWS, ROWS))
    rt, rx, ry, rz = digits(ri)
    ct, cx, cy, cz = digits(ci)

    def kron(time_entry, space_entry):
        out = expand(time_entry, rt, ct, 3, 3)
        for r, c in ((rx, cx), (ry, cy), (rz, cz)):
            out = out * expand(space_entry, r, c, 4, 4)
        return out

    def inverse_of(ref):
        return lambda a, b: (2.0 - ref[a, b]) if a == b else -ref[a, b]

    def plain(ref):
        return lambda a, b: ref[a, b]

    def store_terms(ref, value):
        rows = value.shape[0]
        for i, term in enumerate(split(value)):
            ref[i * rows : (i + 1) * rows, :] = term

    store_terms(j_ref, kron(inverse_of(tb_ref), inverse_of(sb_ref)))

    def columns(n):
        if isinstance(n, int):
            return pl.ds(n * TILE, TILE)
        return pl.ds(pl.multiple_of(n * TILE, TILE), TILE)

    def load(ref, rows, n):
        return jnp.concatenate([ref[2 * n, rows, :], ref[2 * n + 1, rows, :]], axis=1)

    def store(ref, rows, n, value):
        ref[2 * n, rows, :] = value[:, 0:128]
        ref[2 * n + 1, rows, :] = value[:, 128:256]

    def add(ref, rows, n, value):
        store(ref, rows, n, load(ref, rows, n) + value)

    def add_wide(ref, rows, value):
        for n in range(width // TILE):
            add(ref, rows, n, value[:, n * TILE : (n + 1) * TILE])

    def field_tile(s, at):
        return f_ref[pl.ds(s * 24, 24), :, at].reshape(ROWS, TILE)

    def smooth(s, n, source, rnd_in, rnd_out):
        at = columns(n)
        rows = pl.ds(s * ROWS, ROWS)
        terms = split(load(w_ref, rows, n) if source is None else field_tile(s, at))
        if source is not None:
            for i, term in enumerate(terms):
                ft_ref[i, rows, at] = term
        update = product(j_ref, ROWS, terms) * inverse_at(at)
        if rnd_in is not None:
            update = update + load(v_ref.at[rnd_in], rows, n)
        store(v_ref.at[rnd_out], rows, n, update)
        for i, term in enumerate(split(update)):
            vt_ref[i, rows, at] = term

    def inverse_at(at):
        return 1.0 / c_ref[:, at]

    def picked_traces(rnd, s):
        for side in range(2):
            x = 3 * (1 - side)
            rows = [pl.ds(s * ROWS + t * 64 + x * 16, 16) for t in range(3)]
            lhs = jnp.concatenate([vt_ref[i, r, :] for i in range(PICKED) for r in rows], axis=0)
            send_ref[rnd, side, s] = blocks(dot(lhs, pick_ref[side]), 48)
            halo_copy(rnd, side, s).start()

    def tiled(fn):
        for n in range(width // TILE):
            fn(n)

    def loop(count, fn):
        def step(n, carry):
            fn(n)
            return carry

        lax.fori_loop(0, count, step, 0)

    tiles = width // TILE
    for s in (1, 0):
        for h in range(2):
            half_copy(s, h).wait()
        tiled(lambda n: smooth(s, n, f_ref, None, 0))
        if s == 1:
            pl.semaphore_wait(barrier, n_slab + 1)

            @pl.when(slab < n_slab - 1)
            def _():
                prev_copy(0).start()

        picked_traces(0, s)

    k_full = kron(plain(tb_ref), plain(sb_ref))
    same_t, same_x, same_y, same_z = rt == ct, rx == cx, ry == cy, rz == cz
    stiff = plain(st_ref)
    l_full = jnp.where(same_y & same_z, expand(stiff, rx, cx, 4, 4), 0.0)
    l_full = l_full + jnp.where(same_x & same_z, expand(stiff, ry, cy, 4, 4), 0.0)
    l_full = l_full + jnp.where(same_x & same_y, expand(stiff, rz, cz, 4, 4), 0.0)
    l_full = jnp.where(same_t, l_full, 0.0)
    store_terms(kl_ref, jnp.concatenate([k_full, l_full], axis=0))

    ci8, cj8 = iotas((8, ROWS))
    gx, gy, gz = ci8 >> 2, (ci8 >> 1) & 1, ci8 & 1
    jt, jx, jy, jz = digits(cj8)
    sr = plain(sr_ref)
    time_row = expand(lambda a, b: tr_ref[0, b], ci8 * 0, jt, 1, 3)
    by_dim = [expand(sr, g, j, 2, 4) for g, j in ((gx, jx), (gy, jy), (gz, jz))]
    restrict = time_row * by_dim[0] * by_dim[1] * by_dim[2]
    m3 = [
        jnp.dot(restrict, k_full, precision=HIGHEST, preferred_element_type=F32),
        jnp.dot(restrict, l_full, precision=HIGHEST, preferred_element_type=F32),
    ]
    for face in range(6):
        d, node = face // 2, face % 2 * 3
        at_face = expand(lambda a, b: sr_ref[a, node], (gx, gy, gz)[d], cj8 * 0, 2, 1)
        value = time_row * jnp.where((jx, jy, jz)[d] == 3 - node, at_face, 0.0)
        for other in range(3):
            if other != d:
                value = value * by_dim[other]
        m3.append(value)
    last = jnp.where(jt == 2, tr_ref[0, 0], 0.0) * by_dim[0] * by_dim[1] * by_dim[2]
    m3.append(last)
    m3.append(jnp.zeros((8, ROWS), F32))
    store_terms(m3_ref, jnp.concatenate(m3, axis=0))
    store_terms(r_ref, jnp.concatenate([restrict, jnp.zeros((8, ROWS), F32)], axis=0))

    def build_hot(k):
        base = k * 64
        for face in range(6):
            hot_ref[face, pl.ds(pl.multiple_of(base, 64), 64), :] = hot_rows(
                nb_ref[face : face + 1, :] - base
            )

    loop(width // 64, build_hot)

    def build_ghost(k):
        base = k * 64
        for side in range(2):
            first = width + side * ghosts
            ghost_hot_ref[side, pl.ds(pl.multiple_of(base, 64), 64), :] = hot_rows(
                nb_ref[side : side + 1, :] - (base + first)
            )

    loop(ghosts // 64, build_ghost)

    def residual_tile(rnd, s, n):
        at = columns(n)
        rows = pl.ds(s * ROWS, ROWS)
        c = c_ref[:, at]
        out = product(kl_ref, 2 * ROWS, [vt_ref[i, rows, at] for i in range(TERMS)])
        k_part, l_part = out[0:ROWS], out[ROWS:]
        store(w_ref, rows, n, field_tile(s, at) - c * k_part - l_part)
        if s == 1:
            add(w_ref, pl.ds(ROWS, 64), n, UPWIND * c * load(v_ref.at[rnd], pl.ds(128, 64), n))

    def face_rows(face):
        d, node = face // 2, face % 2 * 3
        if d == 0:
            return [pl.ds(st * 64 + node * 16, 16) for st in range(6)]
        if d == 1:
            return [pl.ds(node * 4 + z, 24, stride=16) for z in range(4)]
        return [pl.ds(node, 96, stride=4)]

    def stage_traces(rnd, n):
        at = columns(n)
        for face in range(6):
            trace = jnp.concatenate([load(v_ref.at[rnd], r, n) for r in face_rows(face ^ 1)], axis=0)
            for i, term in enumerate(split(trace, PICKED)):
                lhs_ref[face, i * 96 : (i + 1) * 96, at] = term

    def couple(face):
        out = PENALTY * blocks(dot(lhs_ref[face], hot_ref[face]), 96)
        first = 0
        for r in face_rows(face):
            add_wide(w_ref, r, out[first : first + r.size])
            first += r.size

    def upwind(rnd, n):
        add(w_ref, pl.ds(0, 64), n, UPWIND * c_ref[:, columns(n)] * load(prev_ref.at[rnd], pl.ds(0, 64), n))

    def couple_ghosts(rnd, side, s):
        lhs = jnp.concatenate(split(recv_ref[rnd, side, s], PICKED), axis=0)
        out = PENALTY * blocks(dot(lhs, ghost_hot_ref[side]), 48)
        for t in range(3):
            r = pl.ds(s * ROWS + t * 64 + side * 48, 16)
            add_wide(w_ref, r, out[16 * t : 16 * t + 16])

    ys = {}
    for rnd in range(2):
        for s in range(2):
            tiled(lambda n: residual_tile(rnd, s, n))
        tiled(lambda n: stage_traces(rnd, n))
        for face in range(6):
            couple(face)
        for s in (1, 0):
            if s == 0:

                @pl.when(slab > 0)
                def _():
                    prev_copy(rnd).wait_recv()

                tiled(lambda n: upwind(rnd, n))
            for side in range(2):
                halo_copy(rnd, side, s).wait_recv()
                couple_ghosts(rnd, side, s)
            tiled(lambda n: smooth(s, n, None, rnd, rnd + 1))
            if rnd == 0:
                if s == 1:

                    @pl.when(slab < n_slab - 1)
                    def _():
                        prev_copy(1).start()

                picked_traces(1, s)
            else:
                out_copy(s).start()
                rows = pl.ds(s * ROWS, ROWS)
                ys[s] = product(m3_ref, 80, [vt_ref[i, rows, :] for i in range(TERMS)])
                if s == 1:
                    sprev3_ref[...] = ys[1][64:72]

                    @pl.when(slab < n_slab - 1)
                    def _():
                        prev3_copy.start()

    summed = ys[0] + ys[1]

    def narrow_terms(value):
        terms = [term.astype(F32) for term in split(value)]
        return jnp.concatenate(terms + [jnp.zeros_like(value)], axis=0).astype(BF16)

    for face in range(6):
        q_ref[:, pl.ds(face * width, width)] = narrow_terms(
            summed[16 + 8 * face : 24 + 8 * face]
        )
    for side in range(2):
        out = dot(q_ref[:, pl.ds(side * width, width)], pick_ref[side])
        send3_ref[side] = blocks(out[0:24], 8)
        halo3_copy(side).start()
    rf = None
    for s in range(2):
        rows = pl.ds(s * ROWS, ROWS)
        term = product(r_ref, 16, [ft_ref[i, rows, :] for i in range(TERMS)])
        rf = term[0:8] if rf is None else rf + term[0:8]
    grouped = rf - summed[8:16]
    grouped = grouped + coef * (UPWIND * ys[0][64:72] - summed[0:8])
    local = None
    for face in range(6):
        term = dot(q_ref[:, pl.ds(face * width, width)], hot_ref[face])
        local = term if local is None else local + term
    for side in range(2):
        halo3_copy(side).wait_recv()
        local = local + dot(narrow_terms(recv3_ref[side]), ghost_hot_ref[side])
    grouped = grouped + PENALTY * blocks(local[0:24], 8)

    @pl.when(slab > 0)
    def _():
        prev3_copy.wait_recv()

    grouped = grouped + UPWIND * coef * prev3_ref[...]

    ai, aj = iotas((8, 8))
    cs = plain(cs_ref)
    smoother = expand(cs, ai >> 2, aj >> 2, 2, 2)
    smoother = smoother * expand(cs, (ai >> 1) & 1, (aj >> 1) & 1, 2, 2)
    smoother = smoother * expand(cs, ai & 1, aj & 1, 2, 2)
    offset = jnp.dot(smoother, grouped * inverse, precision=HIGHEST, preferred_element_type=F32)
    offset_ref[...] = offset
    for step in range(1, n_slab):

        @pl.when(slab < n_slab - step)
        def _():
            coarse_copy(step).start()

    for step in range(1, n_slab):

        @pl.when(slab >= step)
        def _():
            coarse_copy(step).wait_recv()

    state = coarse_ref[n_slab - 2]
    for step in range(n_slab - 2, -1, -1):
        term = coarse_ref[step - 1] if step else offset
        state = term + COARSE_UPWIND * jnp.dot(
            smoother, state, precision=HIGHEST, preferred_element_type=F32
        )

    state_ref[...] = state

    for s in range(2):
        out_copy(s).wait()
    for rnd in range(2):
        for side in range(2):
            for s in range(2):
                halo_copy(rnd, side, s).wait_send()
    for side in range(2):
        halo3_copy(side).wait_send()

    @pl.when(slab < n_slab - 1)
    def _():
        prev_copy(0).wait_send()
        prev_copy(1).wait_send()
        prev3_copy.wait_send()

    for step in range(1, n_slab):

        @pl.when(slab < n_slab - step)
        def _():
            coarse_copy(step).wait_send()


def correct(v_ref, state_ref, tr_ref, sr_ref, o_ref, in_ref, sum_ref, in_sem, out_sem):
    def in_copy(s):
        rows = pl.ds(s * ROWS, ROWS)
        return pltpu.make_async_copy(v_ref.at[:, rows, :], in_ref.at[:, rows, :], in_sem.at[s])

    def out_copy(s, h):
        return pltpu.make_async_copy(
            sum_ref.at[pl.ds(s * 24, 24), pl.ds(4 * h, 4), :],
            o_ref.at[pl.ds(s * 24, 24), h],
            out_sem.at[s, h],
        )

    for s in range(2):
        in_copy(s).start()
    pi, pk = iotas((ROWS, 8))
    pt, px, py, pz = digits(pi)
    spread = expand(lambda a, b: tr_ref[0, a], pt, pk * 0, 3, 1)
    for r, g in ((px, pk >> 2), (py, (pk >> 1) & 1), (pz, pk & 1)):
        spread = spread * expand(lambda a, b: sr_ref[b, a], r, g, 4, 2)
    lifted = jnp.dot(spread, state_ref[...], precision=HIGHEST, preferred_element_type=F32)
    for s in range(2):
        in_copy(s).wait()
        for c in range(v_ref.shape[0]):
            at = slice(c * 128, c * 128 + 128)
            total = in_ref[c, s * ROWS : (s + 1) * ROWS, :] + lifted[:, at]
            sum_ref[s * 24 : (s + 1) * 24, :, at] = total.reshape(24, 8, 128)
        for h in range(2):
            out_copy(s, h).start()
    for s in range(2):
        for h in range(2):
            out_copy(s, h).wait()


def body(
    forcing,
    coefficient,
    neighbours,
    halo_faces,
    time_block,
    space_block,
    stiffness,
    time_restrict,
    space_restrict,
    coarse_smoother,
):
    n_slab, n_space = lax.axis_size("slab"), lax.axis_size("space")
    width, ghosts = coefficient.shape[0], halo_faces.shape[1]
    field = (2 * ROWS, width)
    lanes = (width // 128, 2 * ROWS, 128)
    dma = pltpu.SemaphoreType.DMA
    vmem = pl.BlockSpec(memory_space=pltpu.VMEM)
    hbm = pl.BlockSpec(memory_space=pl.ANY)
    smem = pl.BlockSpec(memory_space=pltpu.SMEM)
    iterate, state = pl.pallas_call(
        functools.partial(kernel, n_slab, n_space),
        out_shape=(
            jax.ShapeDtypeStruct(lanes, F32),
            jax.ShapeDtypeStruct((8, width), F32),
        ),
        in_specs=[hbm] + [vmem] * 3 + [smem] * 6,
        out_specs=(hbm, vmem),
        scratch_shapes=[
            pltpu.VMEM((48, 8, width), F32),
            pltpu.VMEM((3,) + lanes, F32),
            pltpu.VMEM(lanes, F32),
            pltpu.VMEM((TERMS,) + field, BF16),
            pltpu.VMEM((TERMS,) + field, BF16),
            pltpu.VMEM((6, PICKED * 96, width), BF16),
            pltpu.VMEM((6, width, width), BF16),
            pltpu.VMEM((2, width, ghosts), BF16),
            pltpu.VMEM((2, ghosts, width), BF16),
            pltpu.VMEM((TERMS * 2 * ROWS, ROWS), BF16),
            pltpu.VMEM((TERMS * ROWS, ROWS), BF16),
            pltpu.VMEM((TERMS * 80, ROWS), BF16),
            pltpu.VMEM((32, 6 * width), BF16),
            pltpu.VMEM((TERMS * 16, ROWS), BF16),
            pltpu.VMEM((2, 2, 2, 48, ghosts), F32),
            pltpu.VMEM((2, 2, 2, 48, ghosts), F32),
            pltpu.VMEM((2, width // 128, 64, 128), F32),
            pltpu.VMEM((2, 8, ghosts), F32),
            pltpu.VMEM((2, 8, ghosts), F32),
            pltpu.VMEM((8, width), F32),
            pltpu.VMEM((8, width), F32),
            pltpu.VMEM((8, width), F32),
            pltpu.VMEM((n_slab - 1, 8, width), F32),
            dma((2, 2, 2)),
            dma((2, 2, 2)),
            dma((3,)),
            dma((3,)),
            dma((2,)),
            dma((2,)),
            dma((n_slab - 1,)),
            dma((n_slab - 1,)),
            dma((2, 2)),
            dma((2,)),
        ],
        compiler_params=pltpu.CompilerParams(
            collective_id=0, has_side_effects=True, vmem_limit_bytes=58 * 1024 * 1024
        ),
        name="window",
    )(
        forcing.reshape(48, 2, 4, width),
        coefficient.reshape(1, width),
        neighbours,
        halo_faces,
        time_block,
        space_block,
        stiffness,
        time_restrict,
        space_restrict,
        coarse_smoother,
    )
    correction = pl.pallas_call(
        correct,
        out_shape=jax.ShapeDtypeStruct((48, 2, 4, width), F32),
        in_specs=[hbm, vmem, smem, smem],
        out_specs=hbm,
        scratch_shapes=[
            pltpu.VMEM(lanes, F32),
            pltpu.VMEM((48, 8, width), F32),
            dma((2,)),
            dma((2, 2)),
        ],
        compiler_params=pltpu.CompilerParams(vmem_limit_bytes=60 * 1024 * 1024),
        name="correct",
    )(iterate, state, time_restrict, space_restrict)
    return correction.reshape(forcing.shape)


def solution(mesh):
    in_specs = (
        P("slab", None, None, None, None, "space"),
        P("space"),
        P(None, "space"),
        P(None, "space"),
        P(),
        P(),
        P(),
        P(),
        P(),
        P(),
    )
    out_specs = P("slab", None, None, None, None, "space")
    return jax.shard_map(body, mesh=mesh, in_specs=in_specs, out_specs=out_specs, check_vma=False)
```
